32 devices in a mesh: dp: 16 (over z, y, x), group: 2 (over core).
Axes of the slice: x: 2, y: 2, z: 4, core: 2. Of those that a mesh axis runs over, the one named last changes fastest.
Arguments:
- hidden_in: bfloat16 [32768, 768], P(('dp', 'group')), may hold values from -6 to 6
- grad_out: bfloat16 [32768, 768], P(('dp', 'group')), may hold values from -6 to 6
- seq_lengths: int32 [64, 16], P(('dp', 'group')), may hold values from 0 to 512, as said below
- key_mask: int32 [32768], P(('dp', 'group')), may hold values from 0 to 1, as said below
- w_qkv: bfloat16 [768, 2304], P(('dp', 'group')), may hold values from -0.21875 to 0.21875
- b_qv: bfloat16 [1536], P(('dp', 'group')), may hold values from -4 to 4
- w_out: bfloat16 [768, 768], P(('dp', 'group')), may hold values from -1.25 to 1.25
- b_out: bfloat16 [768], P(('dp', 'group')), may hold values from -4 to 4
- ln1_gain: bfloat16 [768], P(('dp', 'group')), may hold values from 0.5 to 1.5
- ln1_bias: bfloat16 [768], P(('dp', 'group')), may hold values from -4 to 4
- w_in: bfloat16 [768, 3072], P(('dp', 'group')), may hold values from -0.21875 to 0.21875
- b_in: bfloat16 [3072], P(('dp', 'group')), may hold values from -4 to 4
- w_fc: bfloat16 [3072, 768], P(('dp', 'group')), may hold values from -0.109375 to 0.109375
- b_fc: bfloat16 [768], P(('dp', 'group')), may hold values from -4 to 4
- ln2_gain: bfloat16 [768], P(('dp', 'group')), may hold values from 0.5 to 1.5
- ln2_bias: bfloat16 [768], P(('dp', 'group')), may hold values from -4 to 4
- adapter_weight: float32 [24576], P(('dp', 'group')), may hold values from -0.6 to 0.6
- adapter_first: float32 [24576], P(('dp', 'group')), may hold values from -112 to 112
- adapter_second: float32 [24576], P(('dp', 'group')), may hold values from 32.768 to 524.288
Outputs:
- hidden_out: bfloat16 [32768, 768], P(('dp', 'group'))
- grad_in: float32 [32768, 768], P(('dp', 'group'))
- new_weight: float32 [24576], P(('dp', 'group'))
- new_first: float32 [24576], P(('dp', 'group'))
- new_second: float32 [24576], P(('dp', 'group'))
The draws below stay inside these ranges and needn't reach their ends.
Inputs may be any that keep to these rules, and one draw needn't show every extreme that they name: `seq_lengths`: row r lists the sequence lengths of window r of 512 tokens (a device holds 2 windows, in order); each row sums to 512 and is either one document of 512 tokens followed by zeros, or 16 sentences of 16 tokens or more. `key_mask`: within each sequence the zeros form a tail of at most a quarter of its length; its first token is 1.
All inputs are finite; a program needn't handle non-finite values.
Results may differ from the reference program's by a relative error of at most 0.013.
Values may be sent and summed in bfloat16 or wider, within the bound.
No kernel may reach another device: no remote copies, remote signals or barrier semaphores. Data moves between devices by JAX's collectives and lax.ppermute only.
A program may use at most 128 MiB of HBM per device.

```python
import math
import jax
import jax.numpy as jnp
from jax import lax

MODEL_WIDTH_SIZE = 768
H = 12
HD = 64
FF = 3072
ADAPTER_RANK = 8
DOC_LEN = 512
SLOTS = 16
SHORT = 16
TOK_DEV = 1024
TOKENS = 32768
WINDOWS = 64


def window_layout(key):
    per_device = TOK_DEV // DOC_LEN
    device_count = WINDOWS // per_device
    key_start, key_cuts, key_pads = jax.random.split(key, 3)
    first_long = jax.random.randint(key_start, (), 0, device_count)
    crowded = max(device_count // 16, 1)
    owner_dev = jnp.arange(WINDOWS) // per_device
    long_rows = (owner_dev - first_long) % device_count < crowded
    spare_tokens = DOC_LEN - SLOTS * SHORT
    cut_points = jnp.sort(jax.random.randint(key_cuts, (WINDOWS, SLOTS - 1), 0, spare_tokens + 1), axis=1)
    cut_edges = jnp.concatenate([jnp.zeros((WINDOWS, 1), jnp.int32), cut_points.astype(jnp.int32), jnp.full((WINDOWS, 1), spare_tokens, jnp.int32)], axis=1)
    short_lengths = SHORT + cut_edges[:, 1:] - cut_edges[:, :-1]
    single = jnp.zeros((WINDOWS, SLOTS), jnp.int32).at[:, 0].set(DOC_LEN)
    lengths = jnp.where(long_rows[:, None], single, short_lengths).astype(jnp.int32)
    seq_ends = jnp.cumsum(lengths, axis=1)
    positions = jnp.arange(DOC_LEN, dtype=jnp.int32)
    slot_ids = jnp.sum((positions[None, :, None] >= seq_ends[:, None, :]).astype(jnp.int32), axis=2)
    padding = jax.random.randint(key_pads, (WINDOWS, SLOTS), 0, lengths // 4 + 1)
    limits = jnp.take_along_axis(seq_ends - padding, slot_ids, axis=1)
    mask_flat = (positions[None, :] < limits).astype(jnp.int32).reshape(WINDOWS * DOC_LEN)
    return (lengths, mask_flat)


def draw_seq_lengths(key, part):
    return window_layout(key)[0]


def draw_key_mask(key, part):
    return window_layout(key)[1]


def draw_adapter_weight(key, part):
    key = jax.random.fold_in(key, 7)
    block_extent = MODEL_WIDTH_SIZE * ADAPTER_RANK
    normal_draw = jnp.clip(jax.random.normal(key, (4 * block_extent,), jnp.float32), -6.0, 6.0)
    scales = jnp.where(jnp.arange(4 * block_extent) < 2 * block_extent, MODEL_WIDTH_SIZE ** (-0.5), 0.1)
    return (normal_draw * scales).astype(jnp.float32)


def levels(key, extent, cuts, low, high):
    factor_of, own = 1.0, jax.random.fold_in(key, 6)
    for dim, blocks in cuts:
        heights = jnp.exp(jax.random.uniform(jax.random.fold_in(own, dim), (blocks,), jnp.float32, low / len(cuts), high / len(cuts)))
        factor_of = factor_of * jnp.repeat(heights, extent[dim] // blocks).reshape([-1 if axis == dim else 1 for axis in range(len(extent))])
    return factor_of


def normal_values(rng, shape, scale, bound, pieces=(), kind=jnp.bfloat16):
    level = levels(rng, shape, pieces, -0.22, 0.18) if pieces else 1.0
    values = jax.random.normal(rng, shape, jnp.float32) * scale * level
    return jnp.minimum(jnp.maximum(values, -bound), bound).astype(kind)


def setup_inputs(seed: int = 0) -> dict:
    seeds = jax.random.split(jax.random.key(seed), 20)
    return {
        "hidden_in": normal_values(seeds[0], (TOKENS, MODEL_WIDTH_SIZE), 1.0, 6.0, ((0, 32),)),
        "grad_out": normal_values(seeds[1], (TOKENS, MODEL_WIDTH_SIZE), 1.0, 6.0, ((0, 32),)),
        "seq_lengths": draw_seq_lengths(jax.random.fold_in(seeds[19], 71), 0),
        "key_mask": draw_key_mask(jax.random.fold_in(seeds[19], 71), 0),
        "w_qkv": normal_values(seeds[4], (MODEL_WIDTH_SIZE, 3 * MODEL_WIDTH_SIZE), MODEL_WIDTH_SIZE ** -0.5, 0.21875, ((0, 32),)),
        "b_qv": normal_values(seeds[5], (2 * MODEL_WIDTH_SIZE,), 0.3, 4.0, ((0, 32),)),
        "w_out": normal_values(seeds[6], (MODEL_WIDTH_SIZE, MODEL_WIDTH_SIZE), (MODEL_WIDTH_SIZE // 32) ** -0.5, 1.25, ((0, 32),)),
        "b_out": normal_values(seeds[7], (MODEL_WIDTH_SIZE,), 0.3, 4.0, ((0, 32),)),
        "ln1_gain": jnp.clip(1.0 + 0.1 * jax.random.normal(seeds[8], (MODEL_WIDTH_SIZE,), jnp.float32), 0.5, 1.5).astype(jnp.bfloat16),
        "ln1_bias": normal_values(seeds[9], (MODEL_WIDTH_SIZE,), 0.3, 4.0, ((0, 32),)),
        "w_in": normal_values(seeds[10], (MODEL_WIDTH_SIZE, FF), MODEL_WIDTH_SIZE ** -0.5, 0.21875, ((0, 32),)),
        "b_in": normal_values(seeds[11], (FF,), 0.3, 4.0, ((0, 32),)),
        "w_fc": normal_values(seeds[12], (FF, MODEL_WIDTH_SIZE), FF ** -0.5, 0.109375, ((0, 32),)),
        "b_fc": normal_values(seeds[13], (MODEL_WIDTH_SIZE,), 0.3, 4.0, ((0, 32),)),
        "ln2_gain": jnp.clip(1.0 + 0.1 * jax.random.normal(seeds[14], (MODEL_WIDTH_SIZE,), jnp.float32), 0.5, 1.5).astype(jnp.bfloat16),
        "ln2_bias": normal_values(seeds[15], (MODEL_WIDTH_SIZE,), 0.3, 4.0, ((0, 32),)),
        "adapter_weight": draw_adapter_weight(jax.random.fold_in(seeds[19], 71), 0),
        "adapter_first": normal_values(seeds[17], (4 * MODEL_WIDTH_SIZE * ADAPTER_RANK,), (0.1 * TOKENS ** 0.5), 112.0, ((0, 32),), jnp.float32),
        "adapter_second": jnp.clip(jnp.exp(math.log(524.288) - 2.7725887 * jax.random.uniform(seeds[18], (4 * MODEL_WIDTH_SIZE * ADAPTER_RANK,), jnp.float32) ** levels(seeds[18], (4 * MODEL_WIDTH_SIZE * ADAPTER_RANK,), ((0, 32),), -0.2, 0.2)), 32.768, 524.288),
    }


@jax.custom_vjp
def low(v):
    return lax.optimization_barrier(v.astype(jnp.bfloat16)).astype(jnp.float32)

@jax.custom_vjp
def low_back(v):
    return v

def low_keep(v):
    return (low(v), None)

def low_pass(kept, grad):
    return (grad,)

def back_keep(v):
    return (v, None)

def back_low(kept, grad):
    return (low(grad),)
low.defvjp(low_keep, low_pass)
low_back.defvjp(back_keep, back_low)
norm_eps = 1e-05
low_rank_scale = 2.0
masked_score = -1e+30
beta_one = 0.9
beta_two = 0.999
adam_eps = 1e-08
adam_step = 100.0
decay_rate = 0.01
rate_first = 0.002
rate_second = 0.032

def matrix_product(left, right):
    return jnp.dot(left, right, precision=lax.Precision.HIGHEST)

def widen(values):
    return values.astype(jnp.float32)

def normalize(values, norm_gain, offset):
    centre = lax.optimization_barrier(jnp.mean(values, axis=-1, keepdims=True))
    centred = values - centre
    spread = lax.rsqrt(lax.optimization_barrier(jnp.mean(centred * centred, axis=-1, keepdims=True)) + norm_eps)
    return centred * spread * norm_gain + offset

def window_layer(frozen, adapters, hidden, slot_ids, key_valid):
    w_qkv, query_up_bias, value_up_bias, w_out, b_out, gain_one, offset_one, w_in, b_in, w_fc, b_fc, gain_two, offset_two = frozen
    block_extent = MODEL_WIDTH_SIZE * ADAPTER_RANK
    down_both = jnp.concatenate([adapters[:block_extent].reshape(MODEL_WIDTH_SIZE, ADAPTER_RANK), adapters[block_extent:2 * block_extent].reshape(MODEL_WIDTH_SIZE, ADAPTER_RANK)], axis=1)
    query_up_weight = adapters[2 * block_extent:3 * block_extent].reshape(MODEL_WIDTH_SIZE, ADAPTER_RANK)
    value_up_weight = adapters[3 * block_extent:].reshape(MODEL_WIDTH_SIZE, ADAPTER_RANK)
    rank_reduced = low_back(low(matrix_product(hidden, down_both)))
    down_projected = matrix_product(hidden, w_qkv)
    query_rows = down_projected[:, :MODEL_WIDTH_SIZE] + query_up_bias + low_rank_scale * matrix_product(rank_reduced[:, :ADAPTER_RANK], query_up_weight.T)
    keys_all = down_projected[:, MODEL_WIDTH_SIZE:2 * MODEL_WIDTH_SIZE]
    value_rows_full = down_projected[:, 2 * MODEL_WIDTH_SIZE:] + value_up_bias + low_rank_scale * matrix_product(rank_reduced[:, ADAPTER_RANK:], value_up_weight.T)
    query_rows = low_back(low(query_rows)).reshape(DOC_LEN, H, HD)
    keys_all = low_back(low(keys_all)).reshape(DOC_LEN, H, HD)
    value_rows_full = low_back(low(value_rows_full)).reshape(DOC_LEN, H, HD)
    scores = jnp.einsum('qhd,khd->hqk', query_rows, keys_all, precision=lax.Precision.HIGHEST) * HD ** (-0.5)
    scores = low_back(scores)
    allowed = (slot_ids[:, None] == slot_ids[None, :]) & (key_valid[None, :] > 0)
    scores = jnp.where(allowed[None], scores, masked_score)
    weights = low(jax.nn.softmax(scores, axis=-1))
    mixed_heads = jnp.einsum('hqk,khd->qhd', weights, value_rows_full, precision=lax.Precision.HIGHEST).reshape(DOC_LEN, MODEL_WIDTH_SIZE)
    mixed_heads = low_back(low(mixed_heads))
    attended = low_back(matrix_product(mixed_heads, w_out) + b_out)
    normed_one = normalize(hidden + attended, gain_one, offset_one)
    pre_active = low_back(matrix_product(low(normed_one), w_in) + b_in)
    branch = low_back(matrix_product(low(jax.nn.gelu(pre_active, approximate=False)), w_fc) + b_fc)
    return normalize(normed_one + branch, gain_two, offset_two)

def reference(hidden_in, grad_out, seq_lengths, key_mask, w_qkv, b_qv, w_out, b_out, ln1_gain, ln1_bias, w_in, b_in, w_fc, b_fc, ln2_gain, ln2_bias, adapter_weight, adapter_first, adapter_second):
    frozen = (widen(w_qkv), widen(b_qv[:MODEL_WIDTH_SIZE]), widen(b_qv[MODEL_WIDTH_SIZE:]), widen(w_out), widen(b_out), widen(ln1_gain), widen(ln1_bias), widen(w_in), widen(b_in), widen(w_fc), widen(b_fc), widen(ln2_gain), widen(ln2_bias))
    seq_ends = jnp.cumsum(seq_lengths, axis=1)
    positions = jnp.arange(DOC_LEN, dtype=jnp.int32)
    slot_ids = lax.optimization_barrier(jnp.sum((positions[None, :, None] >= seq_ends[:, None, :]).astype(jnp.int32), axis=2))
    key_valid = key_mask.reshape(WINDOWS, DOC_LEN)
    hidden = widen(hidden_in).reshape(WINDOWS, DOC_LEN, MODEL_WIDTH_SIZE)

    def forward(hidden_all, master):
        adapters = low(master)

        def one_window(window_item):
            return window_layer(frozen, adapters, window_item[0], window_item[1], window_item[2])
        return lax.map(jax.checkpoint(one_window), (hidden_all, slot_ids, key_valid))
    output, pullback = jax.vjp(forward, hidden, adapter_weight)
    grad_hidden, grad_adapter = pullback(widen(grad_out).reshape(WINDOWS, DOC_LEN, MODEL_WIDTH_SIZE))
    flat_place = jnp.arange(4 * MODEL_WIDTH_SIZE * ADAPTER_RANK)
    step_rates = jnp.where(flat_place >= 2 * MODEL_WIDTH_SIZE * ADAPTER_RANK, rate_second, rate_first)
    new_first = beta_one * adapter_first + (1.0 - beta_one) * grad_adapter
    new_second = beta_two * adapter_second + (1.0 - beta_two) * grad_adapter * grad_adapter
    update = new_first / (1.0 - beta_one ** adam_step) / (jnp.sqrt(new_second / (1.0 - beta_two ** adam_step)) + adam_eps)
    new_weight = adapter_weight - step_rates * (update + decay_rate * adapter_weight)
    return (output.reshape(TOKENS, MODEL_WIDTH_SIZE).astype(jnp.bfloat16), grad_hidden.reshape(TOKENS, MODEL_WIDTH_SIZE), new_weight, new_first, new_second)
```

```python
import functools

import jax
import jax.numpy as jnp
from jax import lax
from jax.experimental import pallas as pl
from jax.experimental.pallas import tpu as pltpu
from jax.sharding import PartitionSpec as P

H = 12
ADAPTER_RANK = 8

norm_eps = 1e-05
low_rank_scale = 2.0
beta_one = 0.9
beta_two = 0.999
adam_eps = 1e-08
adam_step = 100.0
decay_rate = 0.01
rate_first = 0.002
rate_second = 0.032
slope_const = 0.3989422804014327
root_half = 0.7071067811865476
masked = -1e30

half = jnp.bfloat16
wide = jnp.float32
AXES = ("dp", "group")
PAIR = 128
FEAT = 128

NN = (((1,), (0,)), ((), ()))
NT = (((1,), (1,)), ((), ()))
TN = (((0,), (0,)), ((), ()))


def dot(left, right, dims=NN):
    return lax.dot_general(left, right, dims, preferred_element_type=wide)


def params(mib=58):
    return pltpu.CompilerParams(vmem_limit_bytes=mib * 2**20)


def shape(dims, dtype):
    return jax.ShapeDtypeStruct(dims, dtype)


def row_mean(values):
    return jnp.mean(values, axis=-1, keepdims=True)


def project_kernel(x_ref, ga_ref, ad_ref, bias_ref, q_ref, k_ref, v_ref, red_ref, wqkv_ref, wout_ref):
    devices = ga_ref.shape[0]
    rows = wout_ref.shape[0] // devices
    for d in range(devices):
        span = slice(rows * d, rows * d + rows)
        for j in range(3):
            wqkv_ref[j, span, :] = ga_ref[d, rows * j : rows * (j + 1), :]
        wout_ref[span, :] = ga_ref[d, rows * 3 : rows * 4, :]
    x = x_ref[...]
    reduced = dot(x, ad_ref[0:16, :], NT).astype(half)
    red_ref[...] = reduced
    up = ad_ref[16:32, :]
    lane = lax.broadcasted_iota(jnp.int32, reduced.shape, 1)
    zero = jnp.zeros_like(reduced)
    width = x.shape[1]
    bias = bias_ref[...].astype(wide)
    q = dot(x, wqkv_ref[0]) + bias[:, :width]
    q += low_rank_scale * dot(jnp.where(lane < 8, reduced, zero), up)
    q_ref[...] = (q.astype(half).astype(wide) * 0.125).astype(half)
    k_ref[...] = dot(x, wqkv_ref[1]).astype(half)
    v = dot(x, wqkv_ref[2]) + bias[:, width:]
    v += low_rank_scale * dot(jnp.where(lane < 8, zero, reduced), up)
    v_ref[...] = v.astype(half)


def project(x, ga, ad, bias):
    rows, width = x.shape
    return pl.pallas_call(
        project_kernel,
        out_shape=[shape((rows, width), half)] * 3
        + [shape((rows, 16), half), shape((3, width, width), half), shape((width, width), half)],
        compiler_params=params(),
    )(x, ga, ad, bias)


def low_lanes(dims):
    return lax.broadcasted_iota(jnp.int32, dims, 1) < 64


def attend_kernel(q_ref, k_ref, v_ref, fq_ref, fk_ref, mixed_ref, inv_ref, p_ref):
    length = q_ref.shape[0]
    tile = 256
    low = low_lanes((length, PAIR))
    zero = jnp.zeros((length, PAIR), half)
    one = jnp.ones((length, PAIR), half)
    v2 = v_ref[...]
    keys = jnp.concatenate([k_ref[...], fk_ref[0]], axis=1)
    values = [
        jnp.concatenate([jnp.where(low, v2, zero), jnp.where(low, one, zero)], axis=1),
        jnp.concatenate([jnp.where(low, zero, v2), jnp.where(low, zero, one)], axis=1),
    ]
    low_t = low_lanes((tile, PAIR))
    zero_t = jnp.zeros((tile, PAIR), half)
    for c in range(length // tile):
        span = slice(c * tile, (c + 1) * tile)
        q2 = q_ref[span, :]
        fq = fq_ref[0, span, :]
        total = None
        for h in range(2):
            qh = jnp.where(low_t, q2, zero_t) if h == 0 else jnp.where(low_t, zero_t, q2)
            scores = dot(jnp.concatenate([qh, fq], axis=1), keys, NT)
            highest = jnp.max(scores, axis=1, keepdims=True)
            p = jnp.exp(scores - highest).astype(half)
            p_ref[0, 0, h, span, :] = p
            part = dot(p, values[h])
            total = part if total is None else total + part
        inv = 1.0 / total[:, PAIR:]
        mixed_ref[span, :] = (total[:, :PAIR] * inv).astype(half)
        inv_ref[span, :] = inv


def attend(q, k, v, fq, fk):
    rows, width = q.shape
    windows, length, _ = fq.shape
    pairs = width // PAIR
    block = pl.BlockSpec((length, PAIR), lambda w, h: (w, h))
    feat = pl.BlockSpec((1, length, FEAT), lambda w, h: (w, 0, 0))
    return pl.pallas_call(
        attend_kernel,
        grid=(windows, pairs),
        in_specs=[block, block, block, feat, feat],
        out_specs=[block, block, pl.BlockSpec((1, 1, 2, length, length), lambda w, h: (w, h, 0, 0, 0))],
        out_shape=[
            shape((rows, width), half),
            shape((rows, width), wide),
            shape((windows, pairs, 2, length, length), half),
        ],
        compiler_params=params(),
    )(q, k, v, fq, fk)


def attend_back_kernel(q_ref, k_ref, v_ref, g_ref, mixed_ref, p_ref, dq_ref, dk_ref, dv_ref):
    length = q_ref.shape[0]
    low = low_lanes((length, PAIR))
    zero = jnp.zeros((length, PAIR), half)
    zero_w = jnp.zeros((length, PAIR), wide)
    k2, v2, g2 = k_ref[...], v_ref[...], g_ref[...]
    q_t, g_t = q_ref[...].T, g2.T
    prod = g2.astype(wide) * mixed_ref[...].astype(wide)
    dq, dks, dvs = None, [], []
    for h in range(2):
        pick = (lambda a, z: jnp.where(low, a, z)) if h == 0 else (lambda a, z: jnp.where(low, z, a))
        centre = jnp.sum(pick(prod, zero_w), axis=1, keepdims=True)
        d_probs = dot(pick(g2, zero), v2, NT) - centre
        p = p_ref[0, 0, h]
        ds = (p.astype(wide) * d_probs).astype(half)
        part = dot(ds, pick(k2, zero))
        dq = part if dq is None else dq + part
        lanes = slice(64 * h, 64 * h + 64)
        dks.append(dot(q_t[lanes], ds))
        dvs.append(dot(g_t[lanes], p))
    dq_ref[...] = (dq * 0.125).astype(half)
    dk_ref[...] = jnp.concatenate(dks, axis=0).astype(half).T
    dv_ref[...] = jnp.concatenate(dvs, axis=0).astype(half).T


def attend_back(q, k, v, g, mixed, p):
    rows, width = q.shape
    windows, pairs, _, length, _ = p.shape
    block = pl.BlockSpec((length, PAIR), lambda w, h: (w, h))
    return pl.pallas_call(
        attend_back_kernel,
        grid=(windows, pairs),
        in_specs=[block] * 5 + [pl.BlockSpec((1, 1, 2, length, length), lambda w, h: (w, h, 0, 0, 0))],
        out_specs=[block] * 3,
        out_shape=[shape((rows, width), half)] * 3,
        compiler_params=params(),
    )(q, k, v, g, mixed, p)


def norm_one_kernel(mixed_ref, wout_ref, x_ref, vec_ref, unit_ref, spread_ref):
    vec = vec_ref[...].astype(wide)
    r = x_ref[...].astype(wide) + (dot(mixed_ref[...], wout_ref[...]) + vec[0:1])
    centred = r - row_mean(r)
    spread = lax.rsqrt(row_mean(centred * centred) + norm_eps)
    unit_ref[...] = centred * spread
    spread_ref[...] = spread


def norm_one(mixed, wout, x, vec):
    rows, width = x.shape
    tile = 512
    block = pl.BlockSpec((tile, width), lambda i: (i, 0))
    thin = pl.BlockSpec((tile, 1), lambda i: (i, 0))
    return pl.pallas_call(
        norm_one_kernel,
        grid=(rows // tile,),
        in_specs=[block, pl.BlockSpec(wout.shape, lambda i: (0, 0)), block, pl.BlockSpec(vec.shape, lambda i: (0, 0))],
        out_specs=[block, thin],
        out_shape=[shape((rows, width), wide), shape((rows, 1), wide)],
        compiler_params=params(),
    )(mixed, wout, x, vec)


def ffn_in_kernel(unit_ref, gb_ref, vec_ref, bin_ref, act_ref, slope_ref, win_ref):
    devices = gb_ref.shape[0]
    width = win_ref.shape[1]
    rows = width // devices

    @pl.when(pl.program_id(0) == 0)
    def _():
        for d in range(devices):
            for j in range(win_ref.shape[0]):
                win_ref[j, rows * d : rows * (d + 1), :] = gb_ref[d, rows * j : rows * (j + 1), :]

    vec = vec_ref[...].astype(wide)
    normed = (unit_ref[...] * vec[1:2] + vec[2:3]).astype(half)
    for j in range(win_ref.shape[0]):
        cols = slice(j * width, (j + 1) * width)
        pre = dot(normed, win_ref[j]) + bin_ref[:, cols].astype(wide)
        phi = 0.5 * (1.0 + lax.erf(pre * root_half))
        act_ref[:, cols] = (pre * phi).astype(half)
        slope_ref[:, cols] = (phi + pre * jnp.exp(-0.5 * pre * pre) * slope_const).astype(half)


def ffn_in(unit, gb, vec, bias):
    rows, width = unit.shape
    devices, both, _ = gb.shape
    hidden = bias.shape[1]
    parts = hidden // width
    tile = 512
    return pl.pallas_call(
        ffn_in_kernel,
        grid=(rows // tile,),
        in_specs=[
            pl.BlockSpec((tile, width), lambda i: (i, 0)),
            pl.BlockSpec((devices, both // 2, width), lambda i: (0, 1, 0)),
            pl.BlockSpec(vec.shape, lambda i: (0, 0)),
            pl.BlockSpec(bias.shape, lambda i: (0, 0)),
        ],
        out_specs=[
            pl.BlockSpec((tile, hidden), lambda i: (i, 0)),
            pl.BlockSpec((tile, hidden), lambda i: (i, 0)),
            pl.BlockSpec((parts, width, width), lambda i: (0, 0, 0)),
        ],
        out_shape=[
            shape((rows, hidden), half),
            shape((rows, hidden), half),
            shape((parts, width, width), half),
        ],
        compiler_params=params(),
    )(unit, gb, vec, bias)


def middle_kernel(
    act_ref, slope_ref, unit_ref, spread_ref, grad_ref, inv_ref, gb_ref, win_ref, wout_ref, vec_ref,
    out_ref, d_one_ref, g_ref,
):
    vec = vec_ref[...].astype(wide)
    devices, rows, width = gb_ref.shape
    parts = win_ref.shape[0]
    per = width // rows
    unit_one = unit_ref[...]
    branch = None
    for j in range(parts):
        w = gb_ref[per * j : per * (j + 1)].reshape(width, width)
        part = dot(act_ref[:, j * width : (j + 1) * width], w)
        branch = part if branch is None else branch + part
    r = unit_one * vec[1:2] + vec[2:3] + (branch + vec[3:4])
    centred = r - row_mean(r)
    spread = lax.rsqrt(row_mean(centred * centred) + norm_eps)
    unit = centred * spread
    out_ref[...] = (unit * vec[4:5] + vec[5:6]).astype(half)
    e = grad_ref[...].astype(wide) * vec[4:5]
    d_two = spread * (e - row_mean(e) - unit * row_mean(e * unit))
    d_branch = d_two.astype(half)
    d_normed = d_two
    for j in range(parts):
        w = gb_ref[per * j : per * (j + 1)].reshape(width, width)
        d_act = dot(d_branch, w, NT)
        d_pre = (d_act * slope_ref[:, j * width : (j + 1) * width].astype(wide)).astype(half)
        d_normed += dot(d_pre, win_ref[j], NT)
    e = d_normed * vec[1:2]
    d_one = spread_ref[...] * (e - row_mean(e) - unit_one * row_mean(e * unit_one))
    d_one_ref[...] = d_one
    d_mixed = dot(d_one.astype(half), wout_ref[...], NT)
    g_ref[...] = (d_mixed * inv_ref[...]).astype(half)


def middle(act, slope, unit, spread, grad, inv, gb, win, wout, vec):
    rows, width = unit.shape
    devices, both, _ = gb.shape
    hidden = act.shape[1]
    tile = 256
    block = pl.BlockSpec((tile, width), lambda i: (i, 0))
    long = pl.BlockSpec((tile, hidden), lambda i: (i, 0))

    def whole(array):
        return pl.BlockSpec(array.shape, lambda i: (0,) * array.ndim, pipeline_mode=pl.Buffered(1))

    return pl.pallas_call(
        middle_kernel,
        grid=(rows // tile,),
        in_specs=[
            long,
            long,
            block,
            pl.BlockSpec((tile, 1), lambda i: (i, 0)),
            block,
            block,
            pl.BlockSpec((devices, both // 2, width), lambda i: (0, 0, 0), pipeline_mode=pl.Buffered(1)),
            whole(win),
            whole(wout),
            whole(vec),
        ],
        out_specs=[block] * 3,
        out_shape=[shape((rows, width), half), shape((rows, width), wide), shape((rows, width), half)],
        compiler_params=params(),
    )(act, slope, unit, spread, grad, inv, gb, win, wout, vec)


def project_back_kernel(dq_ref, dk_ref, dv_ref, d_one_ref, x_ref, red_ref, wqkv_ref, ad_ref, grad_ref, ga_ref):
    dq, dk, dv = dq_ref[...], dk_ref[...], dv_ref[...]
    down, up = ad_ref[0:16, :], ad_ref[16:32, :]
    row = lax.broadcasted_iota(jnp.int32, up.shape, 0)
    none = jnp.zeros_like(up)
    d_red = dot(dq, jnp.where(row < 8, up, none), NT) + dot(dv, jnp.where(row < 8, none, up), NT)
    d_red = (low_rank_scale * d_red).astype(half)
    grad = d_one_ref[...] + dot(dq, wqkv_ref[0], NT)
    grad += dot(dk, wqkv_ref[1], NT)
    grad += dot(dv, wqkv_ref[2], NT)
    grad_ref[...] = grad + dot(d_red, down)
    red = red_ref[...]
    both = jnp.concatenate(
        [
            dot(d_red, x_ref[...], TN),
            low_rank_scale * dot(red, dq, TN)[0:8],
            low_rank_scale * dot(red, dv, TN)[8:16],
        ],
        axis=0,
    )

    @pl.when(pl.program_id(0) == 0)
    def _():
        ga_ref[...] = both

    @pl.when(pl.program_id(0) > 0)
    def _():
        ga_ref[...] += both


def project_back(dq, dk, dv, d_one, x, red, wqkv, ad):
    rows, width = x.shape
    tile = 512
    block = pl.BlockSpec((tile, width), lambda i: (i, 0))
    return pl.pallas_call(
        project_back_kernel,
        grid=(rows // tile,),
        in_specs=[
            block,
            block,
            block,
            block,
            block,
            pl.BlockSpec((tile, 16), lambda i: (i, 0)),
            pl.BlockSpec(wqkv.shape, lambda i: (0, 0, 0)),
            pl.BlockSpec(ad.shape, lambda i: (0, 0)),
        ],
        out_specs=[block, pl.BlockSpec((32, width), lambda i: (0, 0))],
        out_shape=[shape((rows, width), wide), shape((32, width), wide)],
        compiler_params=params(),
    )(dq, dk, dv, d_one, x, red, wqkv, ad)


def body(
    hidden_in, grad_out, seq_lengths, key_mask, w_qkv, b_qv, w_out, b_out, ln1_gain, ln1_bias,
    w_in, b_in, w_fc, b_fc, ln2_gain, ln2_bias, adapter_weight, adapter_first, adapter_second,
):
    tok_rows, width = hidden_in.shape
    windows = seq_lengths.shape[0]
    length = tok_rows // windows
    rank = ADAPTER_RANK
    own_rows = w_out.shape[0]
    devices = width // own_rows
    ffn_parts = w_in.shape[1] // width
    block_extent = width * rank
    span = adapter_weight.shape[0] // rank
    shards = width // span

    factor = adapter_weight.astype(half).reshape(span, rank).T
    line_a = jnp.concatenate([b_qv, b_out, ln1_gain])
    line_b = jnp.concatenate([ln1_bias, b_fc, ln2_gain, ln2_bias])
    lines = jnp.concatenate([b_in[None], line_a[None], line_b[None], jnp.zeros((rank - 3, span), half)], axis=0)
    small = jnp.concatenate([factor, lines, jnp.zeros((rank, width - 2 * span), half)], axis=1)
    pack_a = jnp.concatenate([w_qkv[:, width * j : width * (j + 1)] for j in range(3)] + [w_out, small], axis=0)
    pack_b = jnp.concatenate([w_fc] + [w_in[:, width * j : width * (j + 1)] for j in range(ffn_parts)], axis=0)
    all_a = lax.all_gather(pack_a, AXES, axis=0, tiled=False)
    all_b = lax.all_gather(pack_b, AXES, axis=0, tiled=False)

    seq_ends = jnp.cumsum(seq_lengths, axis=1)
    positions = jnp.arange(length, dtype=jnp.int32)
    slot_ids = jnp.sum((positions[None, :, None] >= seq_ends[:, None, :]).astype(jnp.int32), axis=2)
    slots = seq_lengths.shape[1]
    lane = jnp.arange(FEAT, dtype=jnp.int32)[None, None, :]
    same = slot_ids[:, :, None] == lane
    padded = (key_mask.reshape(windows, length) == 0)[:, :, None]
    query_feat = jnp.where((lane <= slots) & ~same, 1.0, 0.0).astype(half)
    key_feat = jnp.where(same | ((lane == slots) & padded), masked, 0.0).astype(half)

    small_all = all_a[:, 4 * own_rows :, :]
    factors = small_all[:, :, :span].reshape(4, shards, rank, span)
    factors = jnp.swapaxes(factors, 1, 2).reshape(4 * rank, width)
    bias_in = small_all[:, 0, span : 2 * span].reshape(1, -1)
    row_a = small_all[:, 1, span : 2 * span]
    row_b = small_all[:, 2, span : 2 * span]
    bias_qv = row_a[:, : 2 * own_rows].reshape(1, -1)
    vec = jnp.concatenate(
        [row_a[:, 2 * own_rows :].reshape(devices, 2, own_rows), row_b.reshape(devices, 4, own_rows)], axis=1
    )
    vec = jnp.swapaxes(vec, 0, 1).reshape(6, width)
    vec = jnp.concatenate([vec, jnp.zeros((2, width), half)], axis=0)

    q, k, v, reduced, wqkv, wout = project(hidden_in, all_a, factors, bias_qv)
    mixed, inv, probs = attend(q, k, v, query_feat, key_feat)
    unit_one, spread_one = norm_one(mixed, wout, hidden_in, vec)
    act, slope, win = ffn_in(unit_one, all_b, vec, bias_in)
    hidden_out, d_one, g = middle(act, slope, unit_one, spread_one, grad_out, inv, all_b, win, wout, vec)
    dq, dk, dv = attend_back(q, k, v, g, mixed, probs)
    grad_in, factor_grad = project_back(dq, dk, dv, d_one, hidden_in, reduced, wqkv, factors)

    partial_grad = factor_grad.reshape(4, rank, shards, span).swapaxes(1, 2).reshape(devices, rank, span)
    owned = lax.all_to_all(partial_grad, AXES, 0, 0, tiled=True)
    owned_grad = jnp.sum(owned, axis=0).T.reshape(-1)
    shard_len = owned_grad.shape[0]
    flat_place = lax.axis_index(AXES) * shard_len + jnp.arange(shard_len, dtype=jnp.int32)
    step_rates = jnp.where(flat_place >= 2 * block_extent, rate_second, rate_first)
    new_first = beta_one * adapter_first + (1.0 - beta_one) * owned_grad
    new_second = beta_two * adapter_second + (1.0 - beta_two) * owned_grad * owned_grad
    update = (
        new_first
        / (1.0 - beta_one**adam_step)
        / (jnp.sqrt(new_second / (1.0 - beta_two**adam_step)) + adam_eps)
    )
    new_weight = adapter_weight - step_rates * (update + decay_rate * adapter_weight)
    return (hidden_out, grad_in, new_weight, new_first, new_second)


def solution(mesh):
    rows, line = P(AXES, None), P(AXES)
    return jax.shard_map(
        body,
        mesh=mesh,
        in_specs=(
            rows, rows, rows, line, rows, line, rows, line, line, line,
            rows, line, rows, line, line, line, line, line, line,
        ),
        out_specs=(rows, rows, line, line, line),
        check_vma=False,
    )
```

```python
import functools

import jax
import jax.numpy as jnp
import numpy as np
from jax import lax
from jax.experimental import pallas as pl
from jax.experimental.pallas import tpu as pltpu
from jax.sharding import PartitionSpec as P

H = 12
ADAPTER_RANK = 8

norm_eps = 1e-05
low_rank_scale = 2.0
beta_one = 0.9
beta_two = 0.999
adam_eps = 1e-08
adam_step = 100.0
decay_rate = 0.01
rate_first = 0.002
rate_second = 0.032
slope_const = 0.3989422804014327
root_half = 0.7071067811865476
masked = -1e30

half = jnp.bfloat16
wide = jnp.float32
AXES = ("dp", "group")
WIDTH = 768
PAIR = 128
FEAT = 128

NN = (((1,), (0,)), ((), ()))
NT = (((1,), (1,)), ((), ()))
TN = (((0,), (0,)), ((), ()))


def dot(left, right, dims=NN):
    return lax.dot_general(left, right, dims, preferred_element_type=wide)


def params(mib=58):
    return pltpu.CompilerParams(vmem_limit_bytes=mib * 2**20)


def cost(us):
    return pl.CostEstimate(flops=int(us * 8e8), bytes_accessed=int(us * 2.5e6), transcendentals=0)


def shape(dims, dtype):
    return jax.ShapeDtypeStruct(dims, dtype)


def row_mean(values):
    return jnp.mean(values, axis=-1, keepdims=True)


class Held:
    def __init__(self, array, owner):
        self.array, self.owner = array, owner

    def send(self, to):
        count = self.owner.shape[0]
        pairs = [(i, to(i)) for i in range(count)]
        owner = np.zeros_like(self.owner)
        for i, j in pairs:
            owner[j] = self.owner[i]
        return Held(lax.ppermute(self.array, AXES, pairs), owner)

    def rows_from(self, start):
        part = Held(self.array, self.owner)
        part.start = start
        return part

    start = 0


def join_after(gate, *held):
    arrays = lax.optimization_barrier((gate, *[h.array for h in held]))[1:]
    return join(*[Held(array, h.owner) for array, h in zip(arrays, held)])


def join(*held):
    return Held(
        jnp.concatenate([h.array for h in held], axis=0), np.concatenate([h.owner for h in held], axis=1)
    )


def after(held, *others):
    first, *_ = lax.optimization_barrier((held.array, *[o.array for o in others]))
    return Held(first, held.owner)


def own(array, devices):
    return Held(array[None], np.arange(devices, dtype=np.int32)[:, None])


def other_core(i):
    return i ^ 1


def first_way(i):
    return i ^ (2 if i % 2 == 0 else 4)


def second_way(i):
    return i ^ (4 if i % 2 == 0 else 2)


def along(i):
    return (i + (8 if i % 2 == 0 else -8)) % 32


def up(i):
    return (i + 8) % 32


def down(i):
    return (i - 8) % 32


def across(i):
    return (i + 16) % 32


def gather_attention(pack_a, pack_b):
    a, b = own(pack_a, 32), own(pack_b, 32)
    near = [a.send(up), a.send(down)]
    ways = a.send(first_way)
    far = a.send(across)
    b_ways = b.send(first_way)
    a_own = join(a, ways)
    a_own2 = a_own.send(second_way)
    near = join(*near)
    near_ways = near.send(first_way)
    far_ways = after(far, near_ways).send(first_way)
    near = join(near, after(near_ways, a_own2))
    near2 = near.send(second_way)
    far = join(far, far_ways)
    far2 = far.send(second_way)
    held = [a_own, a_own2, near, far, near2, far2]
    held += [h.send(other_core) for h in held]
    return held, (b, b_ways, far_ways, far2)


class Ring:
    def __init__(self, state):
        b, b_ways, far_ways, far2 = state
        gate = far2.array
        self.held = []
        self.now = after(b, far_ways).send(along)
        self.ways = [join_after(gate, b, b_ways)]
        self.seconds = [self.ways[0].send(second_way)]
        self.waiting = []
        self.now = after(self.now, far2)
        self.turn()

    def turn(self):
        arrived = self.now
        self.now = arrived.send(along)
        self.waiting.append((arrived, arrived.send(first_way)))

    def step(self, token):
        if self.waiting:
            pair = join_after(token, *self.waiting.pop())
            self.ways.append(pair)
            self.seconds.append(pair.send(second_way))
        if self.now is not None:
            self.now = after(self.now, Held(token, None))
            if len(self.ways) < 3:
                self.turn()
            else:
                self.waiting.append((self.now, self.now.send(first_way)))
                self.now = None

    def swap(self, token, count):
        for pair, second in list(zip(self.ways, self.seconds))[len(self.held) // 4 : count]:
            gated = lax.optimization_barrier((token, pair.array, second.array))[1:]
            pair, second = Held(gated[0], pair.owner), Held(gated[1], second.owner)
            self.held += [pair, second, pair.send(other_core), second.send(other_core)]


def everyone(array, devices):
    owner = np.tile(np.arange(devices, dtype=np.int32), (devices, 1))
    return Held(lax.all_gather(array, AXES, axis=0, tiled=False), owner)


def places(held):
    table = np.concatenate([h.owner for h in held], axis=1)
    assert all(sorted(line) == list(range(len(table))) for line in table)
    return lax.dynamic_index_in_dim(jnp.asarray(table, jnp.int32), lax.axis_index(AXES), 0, keepdims=False)


def place_blocks(starts, table_ref, block_refs, all_ref, sems):
    copies = []
    rows = all_ref.shape[1]
    for start, ref in zip(starts, block_refs):
        for b in range(ref.shape[0]):
            i = len(copies)
            source = ref.at[b] if ref.shape[1] == rows else ref.at[b, pl.ds(start, rows)]
            copies.append(pltpu.make_async_copy(source, all_ref.at[table_ref[i]], sems.at[i]))
    return copies


def run(copies):
    for copy in copies:
        copy.start()
    for copy in copies:
        copy.wait()


SCALARS = pl.BlockSpec(memory_space=pltpu.SMEM)
PLACED = pl.BlockSpec(memory_space=pl.ANY)


def pack_kernel(span, wqkv_ref, wout_ref, win_ref, wfc_ref, factor_ref, lines_ref, a_ref, b_ref, one_ref):
    rows, width = wout_ref.shape
    for j in range(3):
        a_ref[rows * j : rows * (j + 1), :] = wqkv_ref[:, width * j : width * (j + 1)]
    rank = ADAPTER_RANK
    count = factor_ref.shape[1]
    lane = lax.broadcasted_iota(jnp.int32, (rank, count), 1)
    row = lax.broadcasted_iota(jnp.int32, (rank, count), 0)
    spread = jnp.where(lane % rank == row, factor_ref[...].astype(half).astype(wide), 0.0).astype(half)
    place = lax.broadcasted_iota(jnp.int32, (count, PAIR), 0) // rank
    take = (place == lax.broadcasted_iota(jnp.int32, (count, PAIR), 1)).astype(wide).astype(half)
    a_ref[3 * rows :, :PAIR] = dot(spread, take).astype(half)
    a_ref[3 * rows :, PAIR : 2 * PAIR] = jnp.zeros((rank, PAIR), half)
    a_ref[3 * rows : 3 * rows + 3, PAIR : PAIR + span] = lines_ref[...]
    a_ref[3 * rows :, 2 * PAIR :] = jnp.zeros((rank, width - 2 * PAIR), half)
    split = wfc_ref.shape[0]
    one_ref[...] = jnp.zeros_like(one_ref)
    for j in range(win_ref.shape[1] // width):
        one_ref[rows * j : rows * (j + 1), :] = win_ref[:, width * j : width * (j + 1)]
    one_ref[split : split + rows, :] = wout_ref[...]
    b_ref[:split, :] = wfc_ref[...]
    b_ref[split:, :] = one_ref[...]


def pack(w_qkv, w_out, w_in, w_fc, factor, lines):
    rows, width = w_out.shape
    one_rows = w_fc.shape[0] + rows
    one_rows += (-one_rows) % 16
    return pl.pallas_call(
        functools.partial(pack_kernel, lines.shape[1]),
        out_shape=[
            shape((3 * rows + ADAPTER_RANK, width), half),
            shape((w_fc.shape[0] + one_rows, width), half),
            shape((one_rows, width), half),
        ],
        compiler_params=params(),
        cost_estimate=cost(2),
    )(w_qkv, w_out, w_in, w_fc, factor, lines)


def unfold(pieces, piece, per):
    devices, rows, lanes = pieces.shape
    width = WIDTH
    part = width // per
    lane = lax.broadcasted_iota(jnp.int32, (lanes, width), 1)
    row = lax.broadcasted_iota(jnp.int32, (lanes, width), 0)
    repeat = (lane % part + piece == row).astype(wide).astype(half)
    spread = dot(pieces.reshape(devices * rows, lanes), repeat).reshape(devices // per, per, rows, width)
    shard = lax.broadcasted_iota(jnp.int32, (per, rows, width), 0)
    place = lax.broadcasted_iota(jnp.int32, (per, rows, width), 2) // part
    return jnp.sum(jnp.where((shard == place)[None], spread, 0.0), axis=1)


def project_kernel(starts, shards, table_ref, x_ref, *refs):
    blocks = len(starts)
    block_refs = refs[:blocks]
    qkv_ref, red_ref, ad_ref, vec_ref, bin_ref, wout_ref, ga_ref, w_ref, bias_ref, sems, sem = refs[blocks:]
    devices = ga_ref.shape[0]
    width = x_ref.shape[1]
    rows = width // devices
    keep = pltpu.make_async_copy(w_ref, wout_ref, sem)

    @pl.when(pl.program_id(0) == 0)
    def _():
        run(place_blocks(starts, table_ref, block_refs, ga_ref, sems))
        for d in range(devices):
            span = slice(rows * d, rows * d + rows)
            for j in range(3):
                w_ref[j, span, :] = ga_ref[d, rows * j : rows * (j + 1), :]
        keep.start()
        small = ga_ref[:, 3 * rows :, :PAIR]
        lines = ga_ref[:, 3 * rows :, PAIR : 2 * PAIR]
        ad_ref[...] = unfold(small, 0, shards).reshape(4 * ADAPTER_RANK, width).astype(half)
        bin_ref[...] = unfold(lines, 0, shards)[:, 0:1].astype(half)
        bias = unfold(lines, 0, devices // 2)[:, 1:2]
        bias_ref[0], bias_ref[1], bias_ref[2] = bias[0], jnp.zeros_like(bias[0]), bias[1]
        vecs = [unfold(lines, rows * j, devices)[0] for j in range(4)]
        vec_ref[...] = jnp.concatenate(
            [vecs[2][1:2], vecs[3][1:2], vecs[0][2:3], vecs[1][2:3], vecs[2][2:3], vecs[3][2:3], vecs[0][0:2]],
            axis=0,
        )

        red_ref[...] = dot(x_ref[...], ad_ref[0:16, :], NT).astype(half)

    j = pl.program_id(0)
    reduced = red_ref[...]
    lane = lax.broadcasted_iota(jnp.int32, reduced.shape, 1)
    own_lanes = jnp.where(lane // 8 * 2 == j, reduced, jnp.zeros_like(reduced))
    wide_row = dot(x_ref[...], w_ref[j]) + bias_ref[j]
    wide_row += low_rank_scale * dot(own_lanes, ad_ref[16:32, :])
    scale = jnp.where(j == 0, 0.125, 1.0)
    qkv_ref[0] = (wide_row.astype(half).astype(wide) * scale).astype(half)

    @pl.when(j == pl.num_programs(0) - 1)
    def _():
        keep.wait()


def constant(dims):
    return pl.BlockSpec(dims, lambda i: (0,) * len(dims))


def project(x, held, table, parts, shards):
    rows, width = x.shape
    devices = held[0].owner.shape[0]
    return pl.pallas_call(
        functools.partial(project_kernel, [h.start for h in held], shards),
        grid=(3,),
        in_specs=[SCALARS, constant(x.shape)] + [PLACED] * len(held),
        out_specs=[
            pl.BlockSpec((1, rows, width), lambda i: (i, 0, 0)),
            constant((rows, 16)),
            constant((4 * ADAPTER_RANK, width)),
            constant((8, width)),
            constant((parts, 1, width)),
            PLACED,
        ],
        out_shape=[
            shape((3, rows, width), half),
            shape((rows, 16), half),
            shape((4 * ADAPTER_RANK, width), half),
            shape((8, width), wide),
            shape((parts, 1, width), half),
            shape((3, width, width), half),
        ],
        scratch_shapes=[
            pltpu.VMEM((devices, 3 * (width // devices) + ADAPTER_RANK, width), half),
            pltpu.VMEM((3, width, width), half),
            pltpu.VMEM((3, 1, width), wide),
            pltpu.SemaphoreType.DMA((devices,)),
            pltpu.SemaphoreType.DMA,
        ],
        compiler_params=params(),
        cost_estimate=cost(8),
    )(table, x, *[h.array for h in held])


STEP = 2


def low_lanes(length):
    return lax.broadcasted_iota(jnp.int32, (length, PAIR), 1) < 64


def apart(pair, low):
    zero = jnp.zeros_like(pair)
    return jnp.concatenate([jnp.where(low, pair, zero), jnp.where(low, zero, pair)], axis=0)


def together(heads, low):
    length = low.shape[0]
    return jnp.where(low, heads[:length], heads[length:])


def attend_kernel(q_ref, k_ref, v_ref, fq_ref, fk_ref, *refs):
    mixed_ref, inv_ref, p_ref = refs[-3:]
    length = q_ref.shape[1]
    low = low_lanes(length)
    one = jnp.ones((length, PAIR), half)
    fq = jnp.concatenate([fq_ref[0], fq_ref[0]], axis=0)

    def scores_of(i):
        lanes = slice(i * PAIR, (i + 1) * PAIR)
        queries = jnp.concatenate([apart(q_ref[0, :, lanes], low), fq], axis=1)
        keys = jnp.concatenate([k_ref[0, :, lanes], fk_ref[0]], axis=1)
        return dot(queries, keys, NT)

    scores = [scores_of(i) for i in range(STEP)]
    for i in range(STEP):
        lanes = slice(i * PAIR, (i + 1) * PAIR)
        highest = jnp.max(scores[i], axis=1, keepdims=True)
        p = jnp.exp(scores[i] - highest).astype(half)
        p_ref[0, i] = p
        total = dot(p, jnp.concatenate([v_ref[0, :, lanes], one], axis=1))
        inv = together(1.0 / total[:, PAIR:], low)
        mixed_ref[:, lanes] = (together(total[:, :PAIR], low) * inv).astype(half)
        inv_ref[:, lanes] = inv


def attend(window, qkv, fq, fk, before):
    _, rows, width = qkv.shape
    windows, length, _ = fq.shape
    pairs = width // PAIR
    block = pl.BlockSpec((length, STEP * PAIR), lambda h: (window, h))
    feat = pl.BlockSpec((1, length, FEAT), lambda h: (window, 0, 0))
    heads = [pl.BlockSpec((1, length, STEP * PAIR), lambda h, j=j: (j, window, h)) for j in range(3)]
    return pl.pallas_call(
        attend_kernel,
        grid=(pairs // STEP,),
        in_specs=heads + [feat, feat] + [PLACED] * len(before),
        out_specs=[block, block, pl.BlockSpec((1, STEP, 2 * length, length), lambda h: (window, h, 0, 0))],
        out_shape=[
            shape((rows, width), half),
            shape((rows, width), wide),
            shape((windows, pairs, 2 * length, length), half),
        ],
        input_output_aliases={5 + i: i for i in range(len(before))},
        compiler_params=params(),
        cost_estimate=cost(6),
    )(qkv, qkv, qkv, fq, fk, *before)


def attend_back_kernel(
    q_ref, k_ref, v_ref, g_ref, mixed_ref, p_ref, x_ref, red_ref, ad_ref, d_ref, d_red_ref, out_ref, sum_ref, total_ref
):
    length = q_ref.shape[1]
    low = low_lanes(length)
    w, h = pl.program_id(0), pl.program_id(1)
    last = h == pl.num_programs(1) - 1
    row = lax.broadcasted_iota(jnp.int32, (16, PAIR), 0)
    red = red_ref[...]
    zero = jnp.zeros((16, PAIR), half)

    def d_probs_of(i):
        lanes = slice(i * PAIR, (i + 1) * PAIR)
        g2 = g_ref[:, lanes]
        prod = g2.astype(wide) * mixed_ref[:, lanes].astype(wide)
        centre = jnp.sum(apart(prod, low), axis=1, keepdims=True)
        return dot(apart(g2, low), v_ref[0, :, lanes], NT), centre

    d_probs = [d_probs_of(i) for i in range(STEP)]
    d_red = None
    grads = []
    for i in range(STEP):
        lanes = slice(i * PAIR, (i + 1) * PAIR)
        p = p_ref[0, i]
        raw, centre = d_probs[i]
        ds = (p.astype(wide) * (raw - centre)).astype(half)
        q_t, g_t = q_ref[0, :, lanes].T, g_ref[:, lanes].T
        dv = [dot(g_t[64 * n : 64 * n + 64], p[n * length : (n + 1) * length]) for n in range(2)]
        dk = [dot(q_t[64 * n : 64 * n + 64], ds[n * length : (n + 1) * length]) for n in range(2)]
        dq = (together(dot(ds, k_ref[0, :, lanes]), low) * 0.125).astype(half)
        dv = jnp.concatenate(dv, axis=0).astype(half).T
        d_ref[0, :, lanes] = dq
        d_ref[1, :, lanes] = jnp.concatenate(dk, axis=0).astype(half).T
        d_ref[2, :, lanes] = dv
        both = jnp.concatenate([dq, dv], axis=1)
        up = ad_ref[16:32, pl.ds(pl.multiple_of((h * STEP + i) * PAIR, PAIR), PAIR)]
        up = jnp.concatenate([jnp.where(row < 8, up, zero), jnp.where(row < 8, zero, up)], axis=1)
        part = dot(both, up, NT)
        d_red = part if d_red is None else d_red + part
        grads.append(dot(red, both, TN))

    @pl.when(h == 0)
    def _():
        total_ref[...] = d_red

    @pl.when(h > 0)
    def _():
        total_ref[...] += d_red

    for i in range(STEP):
        cols = pl.ds(pl.multiple_of((h * STEP + i) * PAIR, PAIR), PAIR)
        grad = low_rank_scale * jnp.concatenate([grads[i][0:8, :PAIR], grads[i][8:16, PAIR:]], axis=0)

        @pl.when(w == 0)
        def _():
            sum_ref[16:32, cols] = grad

        @pl.when(w > 0)
        def _():
            sum_ref[16:32, cols] += grad

    @pl.when(last)
    def _():
        d_reduced = (low_rank_scale * total_ref[...]).astype(half)
        d_red_ref[...] = d_reduced
        grad = dot(d_reduced, x_ref[...], TN)

        @pl.when(w == 0)
        def _():
            sum_ref[0:16, :] = grad

        @pl.when(w > 0)
        def _():
            sum_ref[0:16, :] += grad

    @pl.when(last & (w == pl.num_programs(0) - 1))
    def _():
        devices, rank, span = out_ref.shape
        shards = sum_ref.shape[1] // span
        for d in range(devices):
            m, i = d // shards, d % shards
            out_ref[d] = sum_ref[m * rank : (m + 1) * rank, i * span : (i + 1) * span]


def attend_back(qkv, g, mixed, p, x, red, ad, devices):
    _, rows, width = qkv.shape
    windows, pairs, _, length = p.shape
    block = pl.BlockSpec((length, STEP * PAIR), lambda w, h: (w, h))
    heads = [pl.BlockSpec((1, length, STEP * PAIR), lambda w, h, j=j: (j, w, h)) for j in range(3)]
    thin = pl.BlockSpec((length, 16), lambda w, h: (w, 0))
    out = (devices, ADAPTER_RANK, 4 * width // devices)
    return pl.pallas_call(
        attend_back_kernel,
        grid=(windows, pairs // STEP),
        in_specs=heads
        + [
            block,
            block,
            pl.BlockSpec((1, STEP, 2 * length, length), lambda w, h: (w, h, 0, 0)),
            pl.BlockSpec((length, width), lambda w, h: (w, 0)),
            thin,
            pl.BlockSpec(ad.shape, lambda w, h: (0, 0)),
        ],
        out_specs=[
            pl.BlockSpec((3, length, STEP * PAIR), lambda w, h: (0, w, h)),
            thin,
            pl.BlockSpec(out, lambda w, h: (0, 0, 0)),
        ],
        out_shape=[shape((3, rows, width), half), shape((rows, 16), half), shape(out, wide)],
        scratch_shapes=[pltpu.VMEM((4 * ADAPTER_RANK, width), wide), pltpu.VMEM((length, 16), wide)],
        compiler_params=params(),
        cost_estimate=cost(20),
    )(qkv, qkv, qkv, g, mixed, p, x, red, ad)


def feed_kernel(
    specs, table_ref, vec_ref, bin_ref, mixed_in, x_in, grad_in, inv_in, *refs
):
    arrays = 1 + max(i for i, _ in specs[0] + specs[1])
    block_refs = refs[:arrays]
    out_out, d_one_out, g_out = refs[arrays : arrays + 3]
    (
        fc_ref, one_ref, win_ref, wout_ref, mixed_ref, x_ref, grad_ref, inv_ref,
        normed_ref, unit_ref, spread_ref, act_ref, slope_ref, sum_ref, out_ref, sems, in_sems, out_sems,
    ) = refs[arrays + 3 :]
    devices, fc_rows, width = fc_ref.shape
    rows_all = x_ref.shape[0]
    parts = win_ref.shape[0]
    per = devices // parts
    rows = width // devices
    copies = []
    for target, spec in ((one_ref, specs[0]), (fc_ref, specs[1])):
        i = 0
        for k, start in spec:
            ref = block_refs[k]
            for b in range(ref.shape[0]):
                count = target.shape[1]
                source = ref.at[b] if ref.shape[1] == count else ref.at[b, pl.ds(start, count)]
                copies.append(pltpu.make_async_copy(source, target.at[table_ref[i]], sems.at[len(copies)]))
                i += 1
    ins = [
        pltpu.make_async_copy(source, target, in_sems.at[i])
        for i, (source, target) in enumerate(
            ((mixed_in, mixed_ref), (x_in, x_ref), (grad_in, grad_ref), (inv_in, inv_ref))
        )
    ]
    for copy in ins[:2] + copies + ins[2:]:
        copy.start()
    for copy in copies[:devices]:
        copy.wait()
    for d in range(devices):
        span = slice(rows * d, rows * (d + 1))
        for j in range(parts):
            win_ref[j, span, :] = one_ref[d, rows * j : rows * (j + 1), :]
        wout_ref[span, :] = one_ref[d, rows * parts : rows * (parts + 1), :]
    vec = vec_ref[...]
    tile = 256
    tiles = rows_all // tile
    for copy in ins[:2]:
        copy.wait()

    @pl.loop(0, tiles)
    def _(t):
        at = pl.ds(pl.multiple_of(t * tile, tile), tile)
        r = x_ref[at, :].astype(wide) + (dot(mixed_ref[at, :], wout_ref[...]) + vec[0:1])
        centred = r - row_mean(r)
        spread = lax.rsqrt(row_mean(centred * centred) + norm_eps)
        unit = centred * spread
        unit_ref[at, :] = unit
        spread_ref[at, :] = spread
        normed_ref[at, :] = (unit * vec[1:2] + vec[2:3]).astype(half)

    piece = 256

    @pl.loop(0, parts)
    def _(j):
        for n in range(width // piece):
            cols = slice(n * piece, (n + 1) * piece)
            pre = dot(normed_ref[...], win_ref[j, :, cols]) + bin_ref[j, :, cols].astype(wide)
            phi = 0.5 * (1.0 + lax.erf(pre * root_half))
            act_ref[j, :, cols] = (pre * phi).astype(half)
            slope_ref[j, :, cols] = (phi + pre * jnp.exp(-0.5 * pre * pre) * slope_const).astype(half)

    for copy in copies[devices:]:
        copy.wait()

    def second(j):
        return fc_ref[pl.ds(j * per, per)].reshape(width, width)

    sum_ref[...] = dot(act_ref[0], second(0))

    @pl.loop(1, parts)
    def _(j):
        sum_ref[...] += dot(act_ref[j], second(j))

    for copy in ins[2:]:
        copy.wait()
    d_branch_ref = normed_ref

    @pl.loop(0, tiles)
    def _(t):
        at = pl.ds(pl.multiple_of(t * tile, tile), tile)
        r = unit_ref[at, :] * vec[1:2] + vec[2:3] + (sum_ref[at, :] + vec[3:4])
        centred = r - row_mean(r)
        spread = lax.rsqrt(row_mean(centred * centred) + norm_eps)
        unit = centred * spread
        out_ref[at, :] = (unit * vec[4:5] + vec[5:6]).astype(half)
        e = grad_ref[at, :].astype(wide) * vec[4:5]
        d_two = spread * (e - row_mean(e) - unit * row_mean(e * unit))
        sum_ref[at, :] = d_two
        d_branch_ref[at, :] = d_two.astype(half)

    outs = [pltpu.make_async_copy(out_ref, out_out, out_sems.at[0])]
    outs[0].start()

    @pl.loop(0, parts)
    def _(j):
        d_act = dot(d_branch_ref[...], second(j), NT)
        d_pre = (d_act * slope_ref[j].astype(wide)).astype(half)
        sum_ref[...] += dot(d_pre, win_ref[j], NT)

    g_ref = mixed_ref

    @pl.loop(0, tiles)
    def _(t):
        at = pl.ds(pl.multiple_of(t * tile, tile), tile)
        unit_one = unit_ref[at, :]
        e = sum_ref[at, :] * vec[1:2]
        d_one = spread_ref[at, :] * (e - row_mean(e) - unit_one * row_mean(e * unit_one))
        sum_ref[at, :] = d_one
        d_mixed = dot(d_one.astype(half), wout_ref[...], NT)
        g_ref[at, :] = (d_mixed * inv_ref[at, :]).astype(half)

    outs += [
        pltpu.make_async_copy(sum_ref, d_one_out, out_sems.at[1]),
        pltpu.make_async_copy(g_ref, g_out, out_sems.at[2]),
    ]
    for copy in outs[1:]:
        copy.start()
    for copy in outs:
        copy.wait()


def feed(mixed, x, grad, inv, arrays, specs, table, vec, bias, fc_rows, one_rows):
    rows, width = x.shape
    devices = table.shape[0]
    parts = bias.shape[0]
    vmem = pltpu.VMEM
    return pl.pallas_call(
        functools.partial(feed_kernel, specs),
        in_specs=[SCALARS, pl.BlockSpec(memory_space=vmem), pl.BlockSpec(memory_space=vmem)]
        + [PLACED] * (4 + len(arrays)),
        out_specs=[PLACED] * 3,
        out_shape=[shape((rows, width), half), shape((rows, width), wide), shape((rows, width), half)],
        scratch_shapes=[
            vmem((devices, fc_rows, width), half),
            vmem((devices, one_rows, width), half),
            vmem((parts, width, width), half),
            vmem((width, width), half),
            vmem((rows, width), half),
            vmem((rows, width), half),
            vmem((rows, width), half),
            vmem((rows, width), wide),
            vmem((rows, width), half),
            vmem((rows, width), wide),
            vmem((rows, 1), wide),
            vmem((parts, rows, width), half),
            vmem((parts, rows, width), half),
            vmem((rows, width), wide),
            vmem((rows, width), half),
            pltpu.SemaphoreType.DMA((2 * devices,)),
            pltpu.SemaphoreType.DMA((4,)),
            pltpu.SemaphoreType.DMA((3,)),
        ],
        compiler_params=params(60),
        cost_estimate=cost(40),
    )(table, vec, bias, mixed, x, grad, inv, *arrays)


def project_back_kernel(d_ref, w_ref, d_one_ref, d_red_ref, ad_ref, grad_ref):
    j = pl.program_id(0)
    part = dot(d_ref[0], w_ref[0], NT)

    @pl.when(j == 0)
    def _():
        grad_ref[...] = d_one_ref[...] + dot(d_red_ref[...], ad_ref[0:16, :]) + part

    @pl.when(j > 0)
    def _():
        grad_ref[...] += part


def project_back(d_qkv, d_one, d_red, wqkv, ad):
    rows, width = d_one.shape
    single = pl.BlockSpec((rows, width), lambda i: (0, 0), pipeline_mode=pl.Buffered(1))
    return pl.pallas_call(
        project_back_kernel,
        grid=(3,),
        in_specs=[
            pl.BlockSpec((1, rows, width), lambda i: (i, 0, 0)),
            pl.BlockSpec((1, width, width), lambda i: (i, 0, 0)),
            single,
            constant(d_red.shape),
            constant(ad.shape),
        ],
        out_specs=constant((rows, width)),
        out_shape=shape((rows, width), wide),
        compiler_params=params(),
        cost_estimate=cost(8),
    )(d_qkv, wqkv, d_one, d_red, ad)


def body(
    hidden_in, grad_out, seq_lengths, key_mask, w_qkv, b_qv, w_out, b_out, ln1_gain, ln1_bias,
    w_in, b_in, w_fc, b_fc, ln2_gain, ln2_bias, adapter_weight, adapter_first, adapter_second,
):
    tok_rows, width = hidden_in.shape
    windows = seq_lengths.shape[0]
    length = tok_rows // windows
    rank = ADAPTER_RANK
    own_rows = w_out.shape[0]
    devices = width // own_rows
    ffn_parts = w_in.shape[1] // width
    block_extent = width * rank
    span = adapter_weight.shape[0] // rank
    shards = width // span

    line_a = jnp.concatenate([b_qv, b_out, ln1_gain])
    line_b = jnp.concatenate([ln1_bias, b_fc, ln2_gain, ln2_bias])
    lines = jnp.stack([b_in, line_a, line_b])
    pack_a, pack_b, pack_1 = pack(w_qkv, w_out, w_in, w_fc, adapter_weight.reshape(1, -1), lines)

    seq_ends = jnp.cumsum(seq_lengths, axis=1)
    positions = jnp.arange(length, dtype=jnp.int32)
    slot_ids = jnp.sum((positions[None, :, None] >= seq_ends[:, None, :]).astype(jnp.int32), axis=2)
    slots = seq_lengths.shape[1]
    lane = jnp.arange(FEAT, dtype=jnp.int32)[None, None, :]
    same = slot_ids[:, :, None] == lane
    padded = (key_mask.reshape(windows, length) == 0)[:, :, None]
    query_feat = jnp.where((lane <= slots) & ~same, 1.0, 0.0).astype(half)
    key_feat = jnp.where(same | ((lane == slots) & padded), masked, 0.0).astype(half)

    staged = devices == 32
    if staged:
        list_a, state = gather_attention(pack_a, pack_b)
        ring = Ring(state)
    else:
        list_a, list_1, list_2 = [[everyone(p, devices)] for p in (pack_a, pack_1, w_fc)]
    qkv, reduced, factors, vec, bias_in, wqkv = project(hidden_in, list_a, places(list_a), ffn_parts, shards)
    before = ()
    if staged:
        ring.step(reduced)
    for w in range(windows):
        before = attend(w, qkv, query_feat, key_feat, before)
        if staged:
            ring.step(before[0])
            ring.swap(before[0], w + 1)
    mixed, inv, probs = before
    if staged:
        ring.swap(mixed, 4)
        held = ring.held
        arrays = [h.array for h in held]
        specs = [[(i, w_fc.shape[0]) for i in range(len(held))], [(i, 0) for i in range(len(held))]]
    else:
        held, arrays = list_1, [list_1[0].array, list_2[0].array]
        specs = [[(0, 0)], [(1, 0)]]
    hidden_out, d_one, g = feed(
        mixed, hidden_in, grad_out, inv, arrays, specs, places(held), vec, bias_in, w_fc.shape[0], pack_1.shape[0]
    )
    d_qkv, d_reduced, partial_grad = attend_back(qkv, g, mixed, probs, hidden_in, reduced, factors, devices)
    grad_in = project_back(d_qkv, d_one, d_reduced, wqkv, factors)
    owned = lax.all_to_all(partial_grad, AXES, 0, 0, tiled=True)
    owned_grad = jnp.sum(owned, axis=0).T.reshape(-1)
    shard_len = owned_grad.shape[0]
    flat_place = lax.axis_index(AXES) * shard_len + jnp.arange(shard_len, dtype=jnp.int32)
    step_rates = jnp.where(flat_place >= 2 * block_extent, rate_second, rate_first)
    new_first = beta_one * adapter_first + (1.0 - beta_one) * owned_grad
    new_second = beta_two * adapter_second + (1.0 - beta_two) * owned_grad * owned_grad
    update = (
        new_first
        / (1.0 - beta_one**adam_step)
        / (jnp.sqrt(new_second / (1.0 - beta_two**adam_step)) + adam_eps)
    )
    new_weight = adapter_weight - step_rates * (update + decay_rate * adapter_weight)
    return (hidden_out, grad_in, new_weight, new_first, new_second)


def solution(mesh):
    rows, line = P(AXES, None), P(AXES)
    return jax.shard_map(
        body,
        mesh=mesh,
        in_specs=(
            rows, rows, rows, line, rows, line, rows, line, line, line,
            rows, line, rows, line, line, line, line, line, line,
        ),
        out_specs=(rows, rows, line, line, line),
        check_vma=False,
    )
```

```python
import functools

import jax
import jax.numpy as jnp
import numpy as np
from jax import lax
from jax.experimental import pallas as pl
from jax.experimental.pallas import tpu as pltpu
from jax.sharding import PartitionSpec as P

H = 12
ADAPTER_RANK = 8

norm_eps = 1e-05
low_rank_scale = 2.0
beta_one = 0.9
beta_two = 0.999
adam_eps = 1e-08
adam_step = 100.0
decay_rate = 0.01
rate_first = 0.002
rate_second = 0.032
slope_const = 0.3989422804014327
root_half = 0.7071067811865476
half_log2e = -0.7213475204444817
masked = -1e30

half = jnp.bfloat16
wide = jnp.float32
AXES = ("dp", "group")
WIDTH = 768
PAIR = 128
FEAT = 128

NN = (((1,), (0,)), ((), ()))
NT = (((1,), (1,)), ((), ()))
TN = (((0,), (0,)), ((), ()))


def dot(left, right, dims=NN):
    return lax.dot_general(left, right, dims, preferred_element_type=wide)


LIMITS = 28, 24, 56, 30, 30


def params(mib=58):
    return pltpu.CompilerParams(vmem_limit_bytes=mib * 2**20)


def cost(us):
    return pl.CostEstimate(flops=int(us * 8e8), bytes_accessed=int(us * 2.5e6), transcendentals=0)


def shape(dims, dtype):
    return pltpu.HBM(dims, dtype)


def near(dims, dtype):
    return pltpu.VMEM(dims, dtype)


def row_mean(values):
    return jnp.mean(values, axis=-1, keepdims=True)


class Held:
    def __init__(self, array, owner):
        self.array, self.owner = array, owner

    def send(self, to):
        count = self.owner.shape[0]
        pairs = [(i, to(i)) for i in range(count)]
        owner = np.zeros_like(self.owner)
        for i, j in pairs:
            owner[j] = self.owner[i]
        return Held(lax.ppermute(self.array, AXES, pairs), owner)

    def rows_from(self, start):
        part = Held(self.array, self.owner)
        part.start = start
        return part

    start = 0


def join_after(gate, *held):
    arrays = lax.optimization_barrier((gate, *[h.array for h in held]))[1:]
    return join(*[Held(array, h.owner) for array, h in zip(arrays, held)])


def join(*held):
    return Held(
        jnp.concatenate([h.array for h in held], axis=0), np.concatenate([h.owner for h in held], axis=1)
    )


def after(held, *others):
    first, *_ = lax.optimization_barrier((held.array, *[o.array for o in others]))
    return Held(first, held.owner)


def own(array, devices):
    return Held(array[None], np.arange(devices, dtype=np.int32)[:, None])


def other_core(i):
    return i ^ 1


def first_way(i):
    return i ^ (2 if i % 2 == 0 else 4)


def second_way(i):
    return i ^ (4 if i % 2 == 0 else 2)


def along(i):
    return (i + (8 if i % 2 == 0 else -8)) % 32


def up(i):
    return (i + 8) % 32


def down(i):
    return (i - 8) % 32


def across(i):
    return (i + 16) % 32


def gather_attention(pack_a, pack_b):
    a, b = own(pack_a, 32), own(pack_b, 32)
    close = [a.send(up), a.send(down)]
    ways = a.send(first_way)
    far = far_first = a.send(across)
    b_ways = b.send(first_way)
    a_own = join(a, ways)
    a_own2 = a_own.send(second_way)
    close = join(*close)
    close_ways = close.send(first_way)
    far_ways = far.send(first_way)
    close = join(close, close_ways)
    close2 = close.send(second_way)
    far = join(far, far_ways)
    far2 = far.send(second_way)
    held = [a_own, a_own2, close, far, close2, far2]
    held += [h.send(other_core) for h in held]
    return held, (b, b_ways, far_first, far2)


class Ring:
    def __init__(self, state):
        b, b_ways, far, far2 = state
        gate = far2.array
        self.held = []
        self.now = after(b, far).send(along)
        self.ways = [join_after(gate, b, b_ways)]
        self.seconds = [self.ways[0].send(second_way)]
        self.waiting = []
        self.now = after(self.now, far2)
        self.turn()

    def turn(self):
        arrived = self.now
        self.now = arrived.send(along)
        self.waiting.append((arrived, arrived.send(first_way)))

    def step(self, token):
        if self.waiting:
            pair = join_after(token, *self.waiting.pop())
            self.ways.append(pair)
            self.seconds.append(pair.send(second_way))
        if self.now is not None:
            self.now = after(self.now, Held(token, None))
            if len(self.ways) < 3:
                self.turn()
            else:
                self.waiting.append((self.now, self.now.send(first_way)))
                self.now = None

    def swap(self, token, count):
        for pair, second in list(zip(self.ways, self.seconds))[len(self.held) // 4 : count]:
            gated = lax.optimization_barrier((token, pair.array, second.array))[1:]
            pair, second = Held(gated[0], pair.owner), Held(gated[1], second.owner)
            self.held += [pair, second, pair.send(other_core), second.send(other_core)]


def everyone(array, devices):
    owner = np.tile(np.arange(devices, dtype=np.int32), (devices, 1))
    return Held(lax.all_gather(array, AXES, axis=0, tiled=False), owner)


def places(held):
    table = np.concatenate([h.owner for h in held], axis=1)
    assert all(sorted(line) == list(range(len(table))) for line in table)
    return lax.dynamic_index_in_dim(jnp.asarray(table, jnp.int32), lax.axis_index(AXES), 0, keepdims=False)


def place_blocks(table_ref, block_refs, all_ref):
    i = 0
    for ref in block_refs:
        for b in range(ref.shape[0]):
            all_ref[table_ref[i]] = ref[b]
            i += 1


SCALARS = pl.BlockSpec(memory_space=pltpu.SMEM)
PLACED = pl.BlockSpec(memory_space=pl.ANY)
NEAR = pl.BlockSpec(memory_space=pltpu.VMEM)


def pack_kernel(span, wqkv_ref, wout_ref, win_ref, wfc_ref, factor_ref, *refs):
    line_refs, (a_ref, b_ref, one_ref) = refs[:-3], refs[-3:]
    rows, width = wout_ref.shape
    for j in range(3):
        a_ref[rows * j : rows * (j + 1), :] = wqkv_ref[:, width * j : width * (j + 1)]
    rank = ADAPTER_RANK
    count = factor_ref.shape[0]
    lane = lax.broadcasted_iota(jnp.int32, (rank, count), 1)
    row = lax.broadcasted_iota(jnp.int32, (rank, count), 0)
    spread = jnp.where(lane % rank == row, factor_ref[...].reshape(1, count).astype(half).astype(wide), 0.0).astype(half)
    place = lax.broadcasted_iota(jnp.int32, (count, PAIR), 0) // rank
    take = (place == lax.broadcasted_iota(jnp.int32, (count, PAIR), 1)).astype(wide).astype(half)
    a_ref[3 * rows :, :PAIR] = dot(spread, take).astype(half)
    a_ref[3 * rows :, PAIR : 2 * PAIR] = jnp.zeros((rank, PAIR), half)
    for i, line in enumerate(LINES):
        at = PAIR
        for k in line:
            n = line_refs[k].shape[0]
            a_ref[3 * rows + i : 3 * rows + i + 1, at : at + n] = line_refs[k][...].reshape(1, n)
            at += n
    a_ref[3 * rows :, 2 * PAIR :] = jnp.zeros((rank, width - 2 * PAIR), half)
    split = wfc_ref.shape[0]
    one_ref[...] = jnp.zeros_like(one_ref)
    for j in range(win_ref.shape[1] // width):
        one_ref[rows * j : rows * (j + 1), :] = win_ref[:, width * j : width * (j + 1)]
    one_ref[split : split + rows, :] = wout_ref[...]
    b_ref[:split, :] = wfc_ref[...]
    b_ref[split:, :] = one_ref[...]


LINES = (0,), (1, 2, 3), (4, 5, 6, 7)


def pack(w_qkv, w_out, w_in, w_fc, factor, vectors):
    rows, width = w_out.shape
    one_rows = w_fc.shape[0] + rows
    one_rows += (-one_rows) % 16
    return pl.pallas_call(
        functools.partial(pack_kernel, factor.shape[0] // ADAPTER_RANK),
        out_shape=[
            jax.ShapeDtypeStruct((3 * rows + ADAPTER_RANK, width), half),
            jax.ShapeDtypeStruct((w_fc.shape[0] + one_rows, width), half),
            jax.ShapeDtypeStruct((one_rows, width), half),
        ],
        compiler_params=params(),
        cost_estimate=cost(2),
    )(w_qkv, w_out, w_in, w_fc, factor, *vectors)


def unfold(pieces, piece, per):
    devices, rows, lanes = pieces.shape
    width = WIDTH
    part = width // per
    lane = lax.broadcasted_iota(jnp.int32, (lanes, width), 1)
    row = lax.broadcasted_iota(jnp.int32, (lanes, width), 0)
    repeat = (lane % part + piece == row).astype(wide).astype(half)
    spread = dot(pieces.reshape(devices * rows, lanes), repeat).reshape(devices // per, per, rows, width)
    shard = lax.broadcasted_iota(jnp.int32, (per, rows, width), 0)
    place = lax.broadcasted_iota(jnp.int32, (per, rows, width), 2) // part
    return jnp.sum(jnp.where((shard == place)[None], spread, 0.0), axis=1)


def project_kernel(blocks, shards, table_ref, x_ref, *refs):
    block_refs = refs[:blocks]
    qkv_ref, far_ref, red_ref, ad_ref, vec_ref, bin_ref, wout_ref, ga_ref, w_ref, bias_ref, sem, sems = refs[blocks:]
    devices = ga_ref.shape[0]
    width = x_ref.shape[1]
    rows = width // devices
    keep = pltpu.make_async_copy(w_ref, wout_ref, sem)

    @pl.when(pl.program_id(0) == 0)
    def _():
        place_blocks(table_ref, block_refs, ga_ref)
        for d in range(devices):
            span = slice(rows * d, rows * d + rows)
            for j in range(3):
                w_ref[j, span, :] = ga_ref[d, rows * j : rows * (j + 1), :]
        keep.start()
        small = ga_ref[:, 3 * rows :, :PAIR]
        lines = ga_ref[:, 3 * rows :, PAIR : 2 * PAIR]
        ad_ref[...] = unfold(small, 0, shards).reshape(4 * ADAPTER_RANK, width).astype(half)
        bin_ref[...] = unfold(lines, 0, shards)[:, 0:1].astype(half)
        bias = unfold(lines, 0, devices // 2)[:, 1:2]
        bias_ref[0], bias_ref[1], bias_ref[2] = bias[0], jnp.zeros_like(bias[0]), bias[1]
        vecs = [unfold(lines, rows * j, devices)[0] for j in range(4)]
        vec_ref[...] = jnp.concatenate(
            [vecs[2][1:2], vecs[3][1:2], vecs[0][2:3], vecs[1][2:3], vecs[2][2:3], vecs[3][2:3], vecs[0][0:2]],
            axis=0,
        )

        red_ref[...] = dot(x_ref[...], ad_ref[0:16, :], NT).astype(half)

    j = pl.program_id(0)
    reduced = red_ref[...]
    lane = lax.broadcasted_iota(jnp.int32, reduced.shape, 1)
    own_lanes = jnp.where(lane // 8 * 2 == j, reduced, jnp.zeros_like(reduced))
    wide_row = dot(x_ref[...], w_ref[j]) + bias_ref[j]
    wide_row += low_rank_scale * dot(own_lanes, ad_ref[16:32, :])
    scale = jnp.where(j == 0, 0.125, 1.0)
    qkv_ref[j] = (wide_row.astype(half).astype(wide) * scale).astype(half)
    pltpu.make_async_copy(qkv_ref.at[j], far_ref.at[j], sems.at[j]).start()

    @pl.when(j == pl.num_programs(0) - 1)
    def _():
        keep.wait()
        for i in range(3):
            pltpu.make_async_copy(qkv_ref.at[i], far_ref.at[i], sems.at[i]).wait()


def constant(dims):
    return pl.BlockSpec(dims, lambda i: (0,) * len(dims))


def project(x, held, table, parts, shards):
    rows, width = x.shape
    devices = held[0].owner.shape[0]
    return pl.pallas_call(
        functools.partial(project_kernel, len(held), shards),
        grid=(3,),
        in_specs=[SCALARS, NEAR] + [NEAR] * len(held),
        out_specs=[
            NEAR,
            PLACED,
            constant((rows, 16)),
            constant((4 * ADAPTER_RANK, width)),
            constant((8, width)),
            constant((parts, 1, width)),
            PLACED,
        ],
        out_shape=[
            near((3, rows, width), half),
            shape((3, rows, width), half),
            shape((rows, 16), half),
            shape((4 * ADAPTER_RANK, width), half),
            shape((8, width), wide),
            shape((parts, 1, width), half),
            shape((3, width, width), half),
        ],
        scratch_shapes=[
            pltpu.VMEM((devices, 3 * (width // devices) + ADAPTER_RANK, width), half),
            pltpu.VMEM((3, width, width), half),
            pltpu.VMEM((3, 1, width), wide),
            pltpu.SemaphoreType.DMA,
            pltpu.SemaphoreType.DMA((3,)),
        ],
        compiler_params=params(LIMITS[0]),
        cost_estimate=cost(8),
    )(table, x, *[h.array for h in held])


STEP = 2


def low_lanes(length):
    return lax.broadcasted_iota(jnp.int32, (length, PAIR), 1) < 64


def apart(pair, low):
    zero = jnp.zeros_like(pair)
    return jnp.concatenate([jnp.where(low, pair, zero), jnp.where(low, zero, pair)], axis=0)


def together(heads, low):
    length = low.shape[0]
    return jnp.where(low, heads[:length], heads[length:])


def attend_kernel(q_ref, k_ref, v_ref, fq_ref, fk_ref, *refs):
    mixed_ref, inv_ref, p_ref = refs[-3:]
    length = q_ref.shape[1]
    low = low_lanes(length)
    one = jnp.ones((length, PAIR), half)
    fq = jnp.concatenate([fq_ref[0], fq_ref[0]], axis=0)

    def scores_of(i):
        lanes = slice(i * PAIR, (i + 1) * PAIR)
        queries = jnp.concatenate([apart(q_ref[0, :, lanes], low), fq], axis=1)
        keys = jnp.concatenate([k_ref[0, :, lanes], fk_ref[0]], axis=1)
        return dot(queries, keys, NT)

    scores = [scores_of(i) for i in range(STEP)]
    for i in range(STEP):
        lanes = slice(i * PAIR, (i + 1) * PAIR)
        highest = jnp.max(scores[i], axis=1, keepdims=True)
        p = jnp.exp(scores[i] - highest).astype(half)
        p_ref[0, i] = p
        total = dot(p, jnp.concatenate([v_ref[0, :, lanes], one], axis=1))
        inv = together(1.0 / total[:, PAIR:], low)
        mixed_ref[:, lanes] = (together(total[:, :PAIR], low) * inv).astype(half)
        inv_ref[:, lanes] = inv


def attend(window, qkv, fq, fk, before):
    _, rows, width = qkv.shape
    windows, length, _ = fq.shape
    pairs = width // PAIR
    block = pl.BlockSpec((length, STEP * PAIR), lambda h: (window, h))
    feat = pl.BlockSpec((1, length, FEAT), lambda h: (window, 0, 0))
    heads = [pl.BlockSpec((1, length, STEP * PAIR), lambda h, j=j: (j, window, h)) for j in range(3)]
    return pl.pallas_call(
        attend_kernel,
        grid=(pairs // STEP,),
        in_specs=heads + [feat, feat] + [PLACED] * len(before),
        out_specs=[block, block, pl.BlockSpec((1, STEP, 2 * length, length), lambda h: (window, h, 0, 0))],
        out_shape=[
            shape((rows, width), half),
            shape((rows, width), wide),
            shape((windows, pairs, 2 * length, length), half),
        ],
        input_output_aliases={5 + i: i for i in range(len(before))},
        compiler_params=params(LIMITS[1]),
        cost_estimate=cost(6),
    )(qkv, qkv, qkv, fq, fk, *before)


def attend_back_kernel(
    q_ref, k_ref, v_ref, g_ref, mixed_ref, p_ref, x_ref, red_ref, ad_ref, d_ref, d_red_ref, out_ref, sum_ref, keep_ref
):
    length = q_ref.shape[1]
    low = low_lanes(length)
    w, h = pl.program_id(0), pl.program_id(1)
    last = h == pl.num_programs(1) - 1

    def d_probs_of(i):
        lanes = slice(i * PAIR, (i + 1) * PAIR)
        g2 = g_ref[:, lanes]
        prod = g2.astype(wide) * mixed_ref[:, lanes].astype(wide)
        centre = jnp.sum(apart(prod, low), axis=1, keepdims=True)
        return dot(apart(g2, low), v_ref[0, :, lanes], NT), centre

    d_probs = [d_probs_of(i) for i in range(STEP)]
    for i in range(STEP):
        lanes = slice(i * PAIR, (i + 1) * PAIR)
        p = p_ref[0, i]
        raw, centre = d_probs[i]
        ds = (p.astype(wide) * (raw - centre)).astype(half)
        q_t, g_t = q_ref[0, :, lanes].T, g_ref[:, lanes].T

        def own_rows(left, both):
            return jnp.concatenate(
                [dot(left, both[n * length : (n + 1) * length])[64 * n : 64 * n + 64] for n in range(2)], axis=0
            )

        dv = own_rows(g_t, p).astype(half).T
        dk = own_rows(q_t, ds).astype(half).T
        dq = (together(dot(ds, k_ref[0, :, lanes]), low) * 0.125).astype(half)
        d_ref[0, :, lanes] = dq
        d_ref[1, :, lanes] = dk
        d_ref[2, :, lanes] = dv
        cols = pl.ds(pl.multiple_of((h * STEP + i) * PAIR, PAIR), PAIR)
        keep_ref[0, :, cols] = dq
        keep_ref[1, :, cols] = dv

    @pl.when(last)
    def _():
        dq, dv = keep_ref[0], keep_ref[1]
        up, red = ad_ref[16:32, :], red_ref[...]
        row = lax.broadcasted_iota(jnp.int32, up.shape, 0)
        none = jnp.zeros_like(up)
        d_red = dot(dq, jnp.where(row < 8, up, none), NT) + dot(dv, jnp.where(row < 8, none, up), NT)
        d_red = (low_rank_scale * d_red).astype(half)
        d_red_ref[...] = d_red
        grad = jnp.concatenate(
            [
                dot(d_red, x_ref[...], TN),
                low_rank_scale * dot(red, dq, TN)[0:8],
                low_rank_scale * dot(red, dv, TN)[8:16],
            ],
            axis=0,
        )

        @pl.when(w == 0)
        def _():
            sum_ref[...] = grad

        @pl.when(w > 0)
        def _():
            sum_ref[...] += grad

    @pl.when(last & (w == pl.num_programs(0) - 1))
    def _():
        devices, rank, span = out_ref.shape
        shards = sum_ref.shape[1] // span
        for d in range(devices):
            m, i = d // shards, d % shards
            out_ref[d] = sum_ref[m * rank : (m + 1) * rank, i * span : (i + 1) * span]


def attend_back(qkv, g, mixed, p, x, red, ad, devices):
    _, rows, width = qkv.shape
    windows, pairs, _, length = p.shape
    block = pl.BlockSpec((length, STEP * PAIR), lambda w, h: (w, h))
    heads = [pl.BlockSpec((1, length, STEP * PAIR), lambda w, h, j=j: (j, w, h)) for j in range(3)]
    thin = pl.BlockSpec((length, 16), lambda w, h: (w, 0))
    out = (devices, ADAPTER_RANK, 4 * width // devices)
    return pl.pallas_call(
        attend_back_kernel,
        grid=(windows, pairs // STEP),
        in_specs=heads
        + [
            block,
            block,
            pl.BlockSpec((1, STEP, 2 * length, length), lambda w, h: (w, h, 0, 0)),
            pl.BlockSpec((length, width), lambda w, h: (w, 0)),
            thin,
            pl.BlockSpec(ad.shape, lambda w, h: (0, 0)),
        ],
        out_specs=[
            pl.BlockSpec((3, length, STEP * PAIR), lambda w, h: (0, w, h)),
            thin,
            pl.BlockSpec(out, lambda w, h: (0, 0, 0)),
        ],
        out_shape=[shape((3, rows, width), half), shape((rows, 16), half), shape(out, wide)],
        scratch_shapes=[pltpu.VMEM((4 * ADAPTER_RANK, width), wide), pltpu.VMEM((2, length, width), half)],
        compiler_params=params(LIMITS[3]),
        cost_estimate=cost(20),
    )(*[pltpu.with_memory_space_constraint(t, pltpu.HBM) for t in (qkv, qkv, qkv, g, mixed, p, x)], red, ad)


def feed_kernel(specs, table_ref, vec_ref, bin_ref, mixed_ref, x_ref, grad_ref, inv_ref, *refs):
    arrays = 1 + max(i for spec in specs for i, _ in spec)
    block_refs = refs[:arrays]
    out_out, d_one_out, g_out = refs[arrays : arrays + 3]
    (
        wo_ref, one_ref, fc_ref, win_ref, wout_ref,
        normed_ref, unit_ref, act_ref, slope_ref, sum_ref, out_ref, d_pre_ref, sems, out_sems,
    ) = refs[arrays + 3 :]
    devices = fc_ref.shape[0]
    rows_all, width = x_ref.shape
    parts = win_ref.shape[0]
    per = devices // parts
    rows = width // devices
    copies = []
    for n, (target, spec) in enumerate(zip((wo_ref, one_ref, fc_ref), specs)):
        count = target.shape[1]
        some = []
        for k, start in spec:
            ref = block_refs[k]
            for b in range(ref.shape[0]):
                source = ref.at[b] if ref.shape[1] == count else ref.at[b, pl.ds(start, count)]
                i = len(some)
                some.append(pltpu.make_async_copy(source, target.at[table_ref[i]], sems.at[n, i]))
        copies.append(some)
    for copy in copies[0]:
        copy.start()
    vec = vec_ref[...]
    tile = 256
    tiles = [slice(t, t + tile) for t in range(0, rows_all, tile)]
    for copy in copies[0]:
        copy.wait()
    for copy in copies[1]:
        copy.start()
    for d in range(devices):
        wout_ref[rows * d : rows * (d + 1), :] = wo_ref[d, 0:rows, :]
    spreads = []
    for at in tiles:
        r = x_ref[at, :].astype(wide) + (dot(mixed_ref[at, :], wout_ref[...]) + vec[0:1])
        centred = r - row_mean(r)
        spread = lax.rsqrt(row_mean(centred * centred) + norm_eps)
        spreads.append(spread)
        unit = centred * spread
        unit_ref[at, :] = unit
        normed_ref[at, :] = (unit * vec[1:2] + vec[2:3]).astype(half)
    for copy in copies[1]:
        copy.wait()
    for copy in copies[2]:
        copy.start()
    for d in range(devices):
        for j in range(parts):
            win_ref[j, rows * d : rows * (d + 1), :] = one_ref[d, rows * j : rows * (j + 1), :]
    piece = 256
    for j in range(parts):
        for n in range(width // piece):
            cols = slice(n * piece, (n + 1) * piece)
            pre = dot(normed_ref[...], win_ref[j, :, cols]) + bin_ref[j, :, cols].astype(wide)
            phi = 0.5 + 0.5 * lax.erf(pre * root_half)
            act_ref[j, :, cols] = (pre * phi).astype(half)
            slope_ref[j, :, cols] = (phi + (pre * slope_const) * jnp.exp2(pre * pre * half_log2e)).astype(half)

    for copy in copies[2]:
        copy.wait()

    def second(j):
        return fc_ref[pl.ds(j * per, per)].reshape(width, width)

    sum_ref[...] = dot(act_ref[0], second(0))

    @pl.loop(1, parts)
    def _(j):
        sum_ref[...] += dot(act_ref[j], second(j))

    d_branch_ref, g_ref = normed_ref, d_pre_ref
    first = second(0)
    for at in tiles:
        r = unit_ref[at, :] * vec[1:2] + vec[2:3] + (sum_ref[at, :] + vec[3:4])
        centred = r - row_mean(r)
        spread = lax.rsqrt(row_mean(centred * centred) + norm_eps)
        unit = centred * spread
        out_ref[at, :] = (unit * vec[4:5] + vec[5:6]).astype(half)
        e = grad_ref[at, :].astype(wide) * vec[4:5]
        d_two = spread * (e - row_mean(e) - unit * row_mean(e * unit))
        sum_ref[at, :] = d_two
        d_branch = d_two.astype(half)
        d_branch_ref[at, :] = d_branch
        d_pre_ref[at, :] = (dot(d_branch, first, NT) * slope_ref[0, at, :].astype(wide)).astype(half)

    outs = [pltpu.make_async_copy(out_ref, out_out, out_sems.at[0])]
    outs[0].start()
    sum_ref[...] += dot(d_pre_ref[...], win_ref[0], NT)

    @pl.loop(1, parts)
    def _(j):
        d_act = dot(d_branch_ref[...], second(j), NT)
        d_pre = (d_act * slope_ref[j].astype(wide)).astype(half)
        sum_ref[...] += dot(d_pre, win_ref[j], NT)

    for i, at in enumerate(tiles):
        unit_one = unit_ref[at, :]
        e = sum_ref[at, :] * vec[1:2]
        d_one = spreads[i] * (e - row_mean(e) - unit_one * row_mean(e * unit_one))
        sum_ref[at, :] = d_one
        d_mixed = dot(d_one.astype(half), wout_ref[...], NT)
        g_ref[at, :] = (d_mixed * inv_ref[at, :]).astype(half)
        outs.append(pltpu.make_async_copy(sum_ref.at[at], d_one_out.at[at], out_sems.at[1 + 2 * i]))
        outs.append(pltpu.make_async_copy(g_ref.at[at], g_out.at[at], out_sems.at[2 + 2 * i]))
        for copy in outs[-2:]:
            copy.start()
    for copy in outs:
        copy.wait()


def feed(mixed, x, grad, inv, arrays, specs, counts, table, vec, bias):
    rows, width = x.shape
    devices = table.shape[0]
    parts = bias.shape[0]
    vmem = pltpu.VMEM
    return pl.pallas_call(
        functools.partial(feed_kernel, specs),
        in_specs=[SCALARS] + [NEAR] * 6 + [PLACED] * len(arrays),
        out_specs=[PLACED] * 3,
        out_shape=[shape((rows, width), half), shape((rows, width), wide), shape((rows, width), half)],
        scratch_shapes=[vmem((devices, count, width), half) for count in counts]
        + [
            vmem((parts, width, width), half),
            vmem((width, width), half),
            vmem((rows, width), half),
            vmem((rows, width), wide),
            vmem((parts, rows, width), half),
            vmem((parts, rows, width), half),
            vmem((rows, width), wide),
            vmem((rows, width), half),
            vmem((rows, width), half),
            pltpu.SemaphoreType.DMA((3, devices)),
            pltpu.SemaphoreType.DMA((1 + 2 * (rows // 256),)),
        ],
        compiler_params=params(LIMITS[2]),
        cost_estimate=cost(40),
    )(table, vec, bias, mixed, x, grad, inv, *arrays)


def project_back_kernel(d_ref, w_ref, one_ref, d_red_ref, ad_ref, grad_ref):
    grad = one_ref[...] + dot(d_red_ref[...], ad_ref[0:16, :])
    for j in range(3):
        grad += dot(d_ref[j], w_ref[j], NT)
    grad_ref[...] = grad


def project_back(d_qkv, d_one, d_red, wqkv, ad):
    rows, width = d_one.shape
    tile = 512
    block = pl.BlockSpec((tile, width), lambda i: (i, 0))
    return pl.pallas_call(
        project_back_kernel,
        grid=(rows // tile,),
        in_specs=[
            pl.BlockSpec((3, tile, width), lambda i: (0, i, 0)),
            pl.BlockSpec(wqkv.shape, lambda i: (0, 0, 0), pipeline_mode=pl.Buffered(1)),
            block,
            pl.BlockSpec((tile, 16), lambda i: (i, 0)),
            constant(ad.shape),
        ],
        out_specs=block,
        out_shape=shape((rows, width), wide),
        compiler_params=params(LIMITS[4]),
        cost_estimate=cost(8),
    )(*[pltpu.with_memory_space_constraint(t, pltpu.HBM) for t in (d_qkv, wqkv, d_one)], d_red, ad)


def body(
    hidden_in, grad_out, seq_lengths, key_mask, w_qkv, b_qv, w_out, b_out, ln1_gain, ln1_bias,
    w_in, b_in, w_fc, b_fc, ln2_gain, ln2_bias, adapter_weight, adapter_first, adapter_second,
):
    tok_rows, width = hidden_in.shape
    windows = seq_lengths.shape[0]
    length = tok_rows // windows
    rank = ADAPTER_RANK
    own_rows = w_out.shape[0]
    devices = width // own_rows
    ffn_parts = w_in.shape[1] // width
    block_extent = width * rank
    span = adapter_weight.shape[0] // rank
    shards = width // span

    vectors = b_in, b_qv, b_out, ln1_gain, ln1_bias, b_fc, ln2_gain, ln2_bias
    pack_a, pack_b, pack_1 = pack(w_qkv, w_out, w_in, w_fc, adapter_weight, vectors)

    seq_ends = jnp.cumsum(seq_lengths, axis=1)
    positions = jnp.arange(length, dtype=jnp.int32)
    slot_ids = jnp.sum((positions[None, :, None] >= seq_ends[:, None, :]).astype(jnp.int32), axis=2)
    slots = seq_lengths.shape[1]
    lane = jnp.arange(FEAT, dtype=jnp.int32)[None, None, :]
    same = slot_ids[:, :, None] == lane
    padded = (key_mask.reshape(windows, length) == 0)[:, :, None]
    query_feat = jnp.where((lane <= slots) & ~same, 1.0, 0.0).astype(half)
    key_feat = jnp.where(same | ((lane == slots) & padded), masked, 0.0).astype(half)

    staged = devices == 32
    split = w_fc.shape[0]
    if staged:
        list_a, state = gather_attention(pack_a, pack_b)
        ring = Ring(state)
    else:
        lists = [[everyone(p, devices)] for p in (pack_a, pack_1[split:], pack_1[:split], w_fc)]
        list_a = lists[0]
    qkv, qkv_far, reduced, factors, vec, bias_in, wqkv = project(hidden_in, list_a, places(list_a), ffn_parts, shards)
    before = ()
    if staged:
        ring.step(reduced)
    for w in range(windows):
        before = attend(w, qkv, query_feat, key_feat, before)
        if staged:
            ring.step(before[0])
            ring.swap(before[0], w + 1)
    mixed, inv, probs = before
    if staged:
        ring.swap(mixed, 4)
        held = ring.held
        arrays = [h.array for h in held]
        specs = [[(i, start) for i in range(len(held))] for start in (2 * split, split, 0)]
    else:
        held, arrays = lists[1], [h[0].array for h in lists[1:]]
        specs = [[(0, 0)], [(1, 0)], [(2, 0)]]
    counts = pack_1.shape[0] - split, split, split
    hidden_out, d_one, g = feed(
        mixed, hidden_in, grad_out, inv, arrays, specs, counts, places(held), vec, bias_in
    )
    d_qkv, d_reduced, partial_grad = attend_back(qkv_far, g, mixed, probs, hidden_in, reduced, factors, devices)
    grad_in = project_back(d_qkv, d_one, d_reduced, wqkv, factors)
    owned = lax.all_to_all(partial_grad, AXES, 0, 0, tiled=True)
    owned_grad = jnp.sum(owned, axis=0).T.reshape(-1)
    shard_len = owned_grad.shape[0]
    flat_place = lax.axis_index(AXES) * shard_len + jnp.arange(shard_len, dtype=jnp.int32)
    step_rates = jnp.where(flat_place >= 2 * block_extent, rate_second, rate_first)
    new_first = beta_one * adapter_first + (1.0 - beta_one) * owned_grad
    new_second = beta_two * adapter_second + (1.0 - beta_two) * owned_grad * owned_grad
    update = (
        new_first
        / (1.0 - beta_one**adam_step)
        / (jnp.sqrt(new_second / (1.0 - beta_two**adam_step)) + adam_eps)
    )
    new_weight = adapter_weight - step_rates * (update + decay_rate * adapter_weight)
    return (hidden_out, grad_in, new_weight, new_first, new_second)


def solution(mesh):
    rows, line = P(AXES, None), P(AXES)
    return jax.shard_map(
        body,
        mesh=mesh,
        in_specs=(
            rows, rows, rows, line, rows, line, rows, line, line, line,
            rows, line, rows, line, line, line, line, line, line,
        ),
        out_specs=(rows, rows, line, line, line),
        check_vma=False,
    )
```

```python
import functools

import jax
import jax.numpy as jnp
import numpy as np
from jax import lax
from jax.experimental import pallas as pl
from jax.experimental.pallas import tpu as pltpu
from jax.sharding import PartitionSpec as P

H = 12
ADAPTER_RANK = 8

norm_eps = 1e-05
low_rank_scale = 2.0
beta_one = 0.9
beta_two = 0.999
adam_eps = 1e-08
adam_step = 100.0
decay_rate = 0.01
rate_first = 0.002
rate_second = 0.032
slope_const = 0.3989422804014327
root_half = 0.7071067811865476
half_log2e = -0.7213475204444817
masked = -1e30

half = jnp.bfloat16
wide = jnp.float32
AXES = ("dp", "group")
WIDTH = 768
PAIR = 128
FEAT = 128

NN = (((1,), (0,)), ((), ()))
NT = (((1,), (1,)), ((), ()))
TN = (((0,), (0,)), ((), ()))


def dot(left, right, dims=NN):
    return lax.dot_general(left, right, dims, preferred_element_type=wide)


LIMITS = 28, 24, 56, 30, 30


def params(mib=58):
    return pltpu.CompilerParams(vmem_limit_bytes=mib * 2**20)


def cost(us):
    return pl.CostEstimate(flops=int(us * 8e8), bytes_accessed=int(us * 2.5e6), transcendentals=0)


def shape(dims, dtype):
    return pltpu.HBM(dims, dtype)


def near(dims, dtype):
    return pltpu.VMEM(dims, dtype)


def row_mean(values):
    return jnp.mean(values, axis=-1, keepdims=True)


class Held:
    def __init__(self, array, owner):
        self.array, self.owner = array, owner

    def send(self, to):
        count = self.owner.shape[0]
        pairs = [(i, to(i)) for i in range(count)]
        owner = np.zeros_like(self.owner)
        for i, j in pairs:
            owner[j] = self.owner[i]
        return Held(lax.ppermute(self.array, AXES, pairs), owner)

    def rows_from(self, start):
        part = Held(self.array, self.owner)
        part.start = start
        return part

    start = 0


def join_after(gate, *held):
    arrays = lax.optimization_barrier((gate, *[h.array for h in held]))[1:]
    return join(*[Held(array, h.owner) for array, h in zip(arrays, held)])


def join(*held):
    return Held(
        jnp.concatenate([h.array for h in held], axis=0), np.concatenate([h.owner for h in held], axis=1)
    )


def after(held, *others):
    first, *_ = lax.optimization_barrier((held.array, *[o.array for o in others]))
    return Held(first, held.owner)


def own(array, devices):
    return Held(array[None], np.arange(devices, dtype=np.int32)[:, None])


def other_core(i):
    return i ^ 1


def first_way(i):
    return i ^ (2 if i % 2 == 0 else 4)


def second_way(i):
    return i ^ (4 if i % 2 == 0 else 2)


def along(i):
    return (i + (8 if i % 2 == 0 else -8)) % 32


def up(i):
    return (i + 8) % 32


def down(i):
    return (i - 8) % 32


def across(i):
    return (i + 16) % 32


def gather_attention(pack_a, pack_b):
    a, b = own(pack_a, 32), own(pack_b, 32)
    close = [a.send(up), a.send(down)]
    ways = a.send(first_way)
    far = far_first = a.send(across)
    b_ways = b.send(first_way)
    a_own = join(a, ways)
    a_own2 = a_own.send(second_way)
    close = join(*close)
    close_ways = close.send(first_way)
    far_ways = far.send(first_way)
    close = join(close, close_ways)
    close2 = close.send(second_way)
    far = join(far, far_ways)
    far2 = far.send(second_way)
    held = [a_own, a_own2, close, far, close2, far2]
    held += [h.send(other_core) for h in held]
    return held, (b, b_ways, far_first, far2)


class Ring:
    def __init__(self, state):
        b, b_ways, far, far2 = state
        gate = far2.array
        self.held = []
        self.now = after(b, far).send(along)
        self.ways = [join_after(gate, b, b_ways)]
        self.seconds = [self.ways[0].send(second_way)]
        self.waiting = []
        self.now = after(self.now, far2)
        self.turn()

    def turn(self):
        arrived = self.now
        self.now = arrived.send(along)
        self.waiting.append((arrived, arrived.send(first_way)))

    def step(self, token):
        if self.waiting:
            pair = join_after(token, *self.waiting.pop())
            self.ways.append(pair)
            self.seconds.append(pair.send(second_way))
        if self.now is not None:
            self.now = after(self.now, Held(token, None))
            if len(self.ways) < 3:
                self.turn()
            else:
                self.last = [self.now, self.now.send(first_way), self.now.send(second_way)]
                self.now = None

    def end(self, token):
        self.last.append(after(self.last[1], Held(token, None)).send(second_way))
        self.hand_over(token, self.last[:3])
        self.held += [self.last[3], self.last[3].send(other_core)]

    def hand_over(self, token, some):
        arrays = lax.optimization_barrier((token, *[h.array for h in some]))[1:]
        for array, h in zip(arrays, some):
            h = Held(array, h.owner)
            self.held += [h, h.send(other_core)]

    def swap(self, token, count):
        for pair, second in list(zip(self.ways, self.seconds))[len(self.held) // 4 : count]:
            self.hand_over(token, [pair, second])


def everyone(array, devices):
    owner = np.tile(np.arange(devices, dtype=np.int32), (devices, 1))
    return Held(lax.all_gather(array, AXES, axis=0, tiled=False), owner)


def places(held):
    table = np.concatenate([h.owner for h in held], axis=1)
    assert all(sorted(line) == list(range(len(table))) for line in table)
    return jnp.asarray(table, jnp.int32)


def place_blocks(me_ref, table_ref, block_refs, all_ref):
    me = me_ref[0]
    i = 0
    for ref in block_refs:
        for b in range(ref.shape[0]):
            all_ref[table_ref[me, i]] = ref[b]
            i += 1


SCALARS = pl.BlockSpec(memory_space=pltpu.SMEM)
PLACED = pl.BlockSpec(memory_space=pl.ANY)
NEAR = pl.BlockSpec(memory_space=pltpu.VMEM)


def pack_kernel(span, wqkv_ref, wout_ref, win_ref, wfc_ref, factor_ref, *refs):
    line_refs, (a_ref, b_ref, one_ref) = refs[:-3], refs[-3:]
    rows, width = wout_ref.shape
    for j in range(3):
        a_ref[rows * j : rows * (j + 1), :] = wqkv_ref[:, width * j : width * (j + 1)]
    rank = ADAPTER_RANK
    count = factor_ref.shape[0]
    lane = lax.broadcasted_iota(jnp.int32, (rank, count), 1)
    row = lax.broadcasted_iota(jnp.int32, (rank, count), 0)
    spread = jnp.where(lane % rank == row, factor_ref[...].reshape(1, count).astype(half).astype(wide), 0.0).astype(half)
    place = lax.broadcasted_iota(jnp.int32, (count, PAIR), 0) // rank
    take = (place == lax.broadcasted_iota(jnp.int32, (count, PAIR), 1)).astype(wide).astype(half)
    a_ref[3 * rows :, :PAIR] = dot(spread, take).astype(half)
    a_ref[3 * rows :, PAIR : 2 * PAIR] = jnp.zeros((rank, PAIR), half)
    for i, line in enumerate(LINES):
        at = PAIR
        for k in line:
            n = line_refs[k].shape[0]
            a_ref[3 * rows + i : 3 * rows + i + 1, at : at + n] = line_refs[k][...].reshape(1, n)
            at += n
    a_ref[3 * rows :, 2 * PAIR :] = jnp.zeros((rank, width - 2 * PAIR), half)
    split = wfc_ref.shape[0]
    one_ref[...] = jnp.zeros_like(one_ref)
    for j in range(win_ref.shape[1] // width):
        one_ref[rows * j : rows * (j + 1), :] = win_ref[:, width * j : width * (j + 1)]
    one_ref[split : split + rows, :] = wout_ref[...]
    b_ref[:split, :] = wfc_ref[...]
    b_ref[split:, :] = one_ref[...]


LINES = (0,), (1, 2, 3), (4, 5, 6, 7)


def pack(w_qkv, w_out, w_in, w_fc, factor, vectors):
    rows, width = w_out.shape
    one_rows = w_fc.shape[0] + rows
    one_rows += (-one_rows) % 16
    return pl.pallas_call(
        functools.partial(pack_kernel, factor.shape[0] // ADAPTER_RANK),
        out_shape=[
            jax.ShapeDtypeStruct((3 * rows + ADAPTER_RANK, width), half),
            jax.ShapeDtypeStruct((w_fc.shape[0] + one_rows, width), half),
            jax.ShapeDtypeStruct((one_rows, width), half),
        ],
        compiler_params=params(),
        cost_estimate=cost(2),
    )(w_qkv, w_out, w_in, w_fc, factor, *vectors)


def unfold(pieces, piece, per):
    devices, lanes = pieces.shape[0], pieces.shape[-1]
    rows = pieces.shape[1:-1]
    part = WIDTH // per
    lane = lax.broadcasted_iota(jnp.int32, (lanes, WIDTH), 1)
    row = lax.broadcasted_iota(jnp.int32, (lanes, WIDTH), 0)
    repeat = (lane % part + piece == row).astype(wide).astype(half)
    spread = dot(pieces.reshape(-1, lanes), repeat).reshape(devices // per, per, *rows, WIDTH)
    dims = (per, *rows, WIDTH)
    shard = lax.broadcasted_iota(jnp.int32, dims, 0)
    place = lax.broadcasted_iota(jnp.int32, dims, len(dims) - 1) // part
    return jnp.sum(jnp.where((shard == place)[None], spread, 0.0), axis=1)


def project_kernel(blocks, shards, me_ref, table_ref, x_ref, *refs):
    block_refs = refs[:blocks]
    qkv_ref, far_ref, red_ref, ad_ref, vec_ref, bin_ref, wout_ref, ga_ref, w_ref, bias_ref, sem, sems = refs[blocks:]
    devices = ga_ref.shape[0]
    width = x_ref.shape[1]
    rows = width // devices
    keep = pltpu.make_async_copy(w_ref, wout_ref, sem)

    @pl.when(pl.program_id(0) == 0)
    def _():
        place_blocks(me_ref, table_ref, block_refs, ga_ref)
        for d in range(devices):
            span = slice(rows * d, rows * d + rows)
            for j in range(3):
                w_ref[j, span, :] = ga_ref[d, rows * j : rows * (j + 1), :]
        keep.start()
        small = ga_ref[:, 3 * rows :, :PAIR]
        lines = [ga_ref[:, 3 * rows + i, PAIR : 2 * PAIR] for i in range(3)]
        ad_ref[...] = unfold(small, 0, shards).reshape(4 * ADAPTER_RANK, width).astype(half)
        line = unfold(lines[0], 0, shards).astype(half)
        for j in range(bin_ref.shape[0]):
            bin_ref[j] = line[j : j + 1]
        bias = unfold(lines[1], 0, devices // 2)
        bias_ref[0], bias_ref[1], bias_ref[2] = bias[0:1], jnp.zeros_like(bias[0:1]), bias[1:2]
        vecs = [unfold(lines[1], rows * j, devices) for j in (2, 3)]
        vecs += [unfold(lines[2], rows * j, devices) for j in range(4)]
        vec_ref[...] = jnp.concatenate(vecs + vecs[:2], axis=0)

        red_ref[...] = dot(x_ref[...], ad_ref[0:16, :], NT).astype(half)

    j = pl.program_id(0)
    reduced = red_ref[...]
    lane = lax.broadcasted_iota(jnp.int32, reduced.shape, 1)
    own_lanes = jnp.where(lane // 8 * 2 == j, reduced, jnp.zeros_like(reduced))
    wide_row = dot(x_ref[...], w_ref[j]) + bias_ref[j]
    wide_row += low_rank_scale * dot(own_lanes, ad_ref[16:32, :])
    scale = jnp.where(j == 0, 0.125, 1.0)
    qkv_ref[j] = (wide_row.astype(half).astype(wide) * scale).astype(half)
    pltpu.make_async_copy(qkv_ref.at[j], far_ref.at[j], sems.at[j]).start()

    @pl.when(j == pl.num_programs(0) - 1)
    def _():
        keep.wait()
        for i in range(3):
            pltpu.make_async_copy(qkv_ref.at[i], far_ref.at[i], sems.at[i]).wait()


def constant(dims):
    return pl.BlockSpec(dims, lambda i: (0,) * len(dims))


def project(me, x, held, parts, shards):
    rows, width = x.shape
    devices = held[0].owner.shape[0]
    return pl.pallas_call(
        functools.partial(project_kernel, len(held), shards),
        grid=(3,),
        in_specs=[SCALARS, SCALARS, NEAR] + [NEAR] * len(held),
        out_specs=[
            NEAR,
            PLACED,
            constant((rows, 16)),
            constant((4 * ADAPTER_RANK, width)),
            constant((8, width)),
            constant((parts, 1, width)),
            PLACED,
        ],
        out_shape=[
            near((3, rows, width), half),
            shape((3, rows, width), half),
            shape((rows, 16), half),
            shape((4 * ADAPTER_RANK, width), half),
            shape((8, width), wide),
            shape((parts, 1, width), half),
            shape((3, width, width), half),
        ],
        scratch_shapes=[
            pltpu.VMEM((devices, 3 * (width // devices) + ADAPTER_RANK, width), half),
            pltpu.VMEM((3, width, width), half),
            pltpu.VMEM((3, 1, width), wide),
            pltpu.SemaphoreType.DMA,
            pltpu.SemaphoreType.DMA((3,)),
        ],
        compiler_params=params(LIMITS[0]),
        cost_estimate=cost(8),
    )(me, places(held), x, *[h.array for h in held])


STEP = 2


def low_lanes(length):
    return lax.broadcasted_iota(jnp.int32, (length, PAIR), 1) < 64


def apart(pair, low):
    zero = jnp.zeros_like(pair)
    return jnp.concatenate([jnp.where(low, pair, zero), jnp.where(low, zero, pair)], axis=0)


def together(heads, low):
    length = low.shape[0]
    return jnp.where(low, heads[:length], heads[length:])


def attend_kernel(q_ref, k_ref, v_ref, fq_ref, fk_ref, *refs):
    mixed_ref, inv_ref, p_ref = refs[-3:]
    length = q_ref.shape[1]
    low = low_lanes(length)
    one = jnp.ones((length, PAIR), half)
    fq = jnp.concatenate([fq_ref[0], fq_ref[0]], axis=0)

    def scores_of(i):
        lanes = slice(i * PAIR, (i + 1) * PAIR)
        queries = jnp.concatenate([apart(q_ref[0, :, lanes], low), fq], axis=1)
        keys = jnp.concatenate([k_ref[0, :, lanes], fk_ref[0]], axis=1)
        return dot(queries, keys, NT)

    scores = [scores_of(i) for i in range(STEP)]
    for i in range(STEP):
        lanes = slice(i * PAIR, (i + 1) * PAIR)
        highest = jnp.max(scores[i], axis=1, keepdims=True)
        p = jnp.exp(scores[i] - highest).astype(half)
        p_ref[0, i] = p
        total = dot(p, jnp.concatenate([v_ref[0, :, lanes], one], axis=1))
        inv = together(1.0 / total[:, PAIR:], low)
        mixed_ref[:, lanes] = (together(total[:, :PAIR], low) * inv).astype(half)
        inv_ref[:, lanes] = inv


def attend(window, qkv, fq, fk, before):
    _, rows, width = qkv.shape
    windows, length, _ = fq.shape
    pairs = width // PAIR
    block = pl.BlockSpec((length, STEP * PAIR), lambda h: (window, h))
    feat = pl.BlockSpec((1, length, FEAT), lambda h: (window, 0, 0))
    heads = [pl.BlockSpec((1, length, STEP * PAIR), lambda h, j=j: (j, window, h)) for j in range(3)]
    return pl.pallas_call(
        attend_kernel,
        grid=(pairs // STEP,),
        in_specs=heads + [feat, feat] + [PLACED] * len(before),
        out_specs=[block, block, pl.BlockSpec((1, STEP, 2 * length, length), lambda h: (window, h, 0, 0))],
        out_shape=[
            shape((rows, width), half),
            shape((rows, width), wide),
            shape((windows, pairs, 2 * length, length), half),
        ],
        input_output_aliases={5 + i: i for i in range(len(before))},
        compiler_params=params(LIMITS[1]),
        cost_estimate=cost(6),
    )(qkv, qkv, qkv, fq, fk, *before)


def attend_back_kernel(
    q_ref, k_ref, v_ref, g_ref, mixed_ref, p_ref, x_ref, red_ref, ad_ref, d_ref, d_red_ref, out_ref, sum_ref, keep_ref
):
    length = q_ref.shape[1]
    low = low_lanes(length)
    w, h = pl.program_id(0), pl.program_id(1)
    last = h == pl.num_programs(1) - 1

    def d_probs_of(i):
        lanes = slice(i * PAIR, (i + 1) * PAIR)
        g2 = g_ref[:, lanes]
        prod = g2.astype(wide) * mixed_ref[:, lanes].astype(wide)
        centre = jnp.sum(apart(prod, low), axis=1, keepdims=True)
        return dot(apart(g2, low), v_ref[0, :, lanes], NT), centre

    d_probs = [d_probs_of(i) for i in range(STEP)]
    for i in range(STEP):
        lanes = slice(i * PAIR, (i + 1) * PAIR)
        p = p_ref[0, i]
        raw, centre = d_probs[i]
        ds = (p.astype(wide) * (raw - centre)).astype(half)
        q_t, g_t = q_ref[0, :, lanes].T, g_ref[:, lanes].T

        def own_rows(left, both):
            return jnp.concatenate(
                [dot(left, both[n * length : (n + 1) * length])[64 * n : 64 * n + 64] for n in range(2)], axis=0
            )

        dv = own_rows(g_t, p).astype(half).T
        dk = own_rows(q_t, ds).astype(half).T
        dq = (together(dot(ds, k_ref[0, :, lanes]), low) * 0.125).astype(half)
        d_ref[0, :, lanes] = dq
        d_ref[1, :, lanes] = dk
        d_ref[2, :, lanes] = dv
        cols = pl.ds(pl.multiple_of((h * STEP + i) * PAIR, PAIR), PAIR)
        keep_ref[0, :, cols] = dq
        keep_ref[1, :, cols] = dv

    @pl.when(last)
    def _():
        dq, dv = keep_ref[0], keep_ref[1]
        up, red = ad_ref[16:32, :], red_ref[...]
        row = lax.broadcasted_iota(jnp.int32, up.shape, 0)
        none = jnp.zeros_like(up)
        d_red = dot(dq, jnp.where(row < 8, up, none), NT) + dot(dv, jnp.where(row < 8, none, up), NT)
        d_red = (low_rank_scale * d_red).astype(half)
        d_red_ref[...] = d_red
        grad = jnp.concatenate(
            [
                dot(d_red, x_ref[...], TN),
                low_rank_scale * dot(red, dq, TN)[0:8],
                low_rank_scale * dot(red, dv, TN)[8:16],
            ],
            axis=0,
        )

        @pl.when(w == 0)
        def _():
            sum_ref[...] = grad

        @pl.when(w > 0)
        def _():
            sum_ref[...] += grad

    @pl.when(last & (w == pl.num_programs(0) - 1))
    def _():
        devices, rank, span = out_ref.shape
        shards = sum_ref.shape[1] // span
        for d in range(devices):
            m, i = d // shards, d % shards
            out_ref[d] = sum_ref[m * rank : (m + 1) * rank, i * span : (i + 1) * span]


def attend_back(qkv, g, mixed, p, x, red, ad, devices):
    _, rows, width = qkv.shape
    windows, pairs, _, length = p.shape
    block = pl.BlockSpec((length, STEP * PAIR), lambda w, h: (w, h))
    heads = [pl.BlockSpec((1, length, STEP * PAIR), lambda w, h, j=j: (j, w, h)) for j in range(3)]
    thin = pl.BlockSpec((length, 16), lambda w, h: (w, 0))
    out = (devices, ADAPTER_RANK, 4 * width // devices)
    return pl.pallas_call(
        attend_back_kernel,
        grid=(windows, pairs // STEP),
        in_specs=heads
        + [
            block,
            block,
            pl.BlockSpec((1, STEP, 2 * length, length), lambda w, h: (w, h, 0, 0)),
            pl.BlockSpec((length, width), lambda w, h: (w, 0)),
            thin,
            pl.BlockSpec(ad.shape, lambda w, h: (0, 0)),
        ],
        out_specs=[
            pl.BlockSpec((3, length, STEP * PAIR), lambda w, h: (0, w, h)),
            thin,
            pl.BlockSpec(out, lambda w, h: (0, 0, 0)),
        ],
        out_shape=[shape((3, rows, width), half), shape((rows, 16), half), shape(out, wide)],
        scratch_shapes=[pltpu.VMEM((4 * ADAPTER_RANK, width), wide), pltpu.VMEM((2, length, width), half)],
        compiler_params=params(LIMITS[3]),
        cost_estimate=cost(20),
    )(*[pltpu.with_memory_space_constraint(t, pltpu.HBM) for t in (qkv, qkv, qkv, g, mixed, p, x)], red, ad)


def feed_kernel(specs, me_ref, table_ref, vec_ref, bin_ref, mixed_ref, x_ref, grad_ref, inv_ref, *refs):
    arrays = 1 + max(i for spec in specs for i, _ in spec)
    block_refs = refs[:arrays]
    out_out, d_one_out, g_out = refs[arrays : arrays + 3]
    (
        wo_ref, one_ref, fc_ref, win_ref, wout_ref,
        normed_ref, unit_ref, act_ref, slope_ref, sum_ref, out_ref, d_pre_ref, sems, out_sems,
    ) = refs[arrays + 3 :]
    devices = fc_ref.shape[0]
    rows_all, width = x_ref.shape
    parts = win_ref.shape[0]
    per = devices // parts
    rows = width // devices
    me = me_ref[0]
    copies = []
    for n, (target, spec) in enumerate(zip((wo_ref, one_ref, fc_ref), specs)):
        count = target.shape[1]
        some = []
        for k, start in spec:
            ref = block_refs[k]
            for b in range(ref.shape[0]):
                source = ref.at[b] if ref.shape[1] == count else ref.at[b, pl.ds(start, count)]
                i = len(some)
                some.append(pltpu.make_async_copy(source, target.at[table_ref[me, i]], sems.at[n, i]))
        copies.append(some)
    for copy in copies[0]:
        copy.start()
    vec = vec_ref[...]
    tile = 256
    tiles = [slice(t, t + tile) for t in range(0, rows_all, tile)]
    for copy in copies[0]:
        copy.wait()
    for copy in copies[1]:
        copy.start()
    for d in range(devices):
        wout_ref[rows * d : rows * (d + 1), :] = wo_ref[d, 0:rows, :]
    spreads = []
    for at in tiles:
        r = x_ref[at, :].astype(wide) + (dot(mixed_ref[at, :], wout_ref[...]) + vec[0:1])
        centred = r - row_mean(r)
        spread = lax.rsqrt(row_mean(centred * centred) + norm_eps)
        spreads.append(spread)
        unit = centred * spread
        unit_ref[at, :] = unit
        normed_ref[at, :] = (unit * vec[1:2] + vec[2:3]).astype(half)
    for copy in copies[1]:
        copy.wait()
    for copy in copies[2]:
        copy.start()
    for d in range(devices):
        for j in range(parts):
            win_ref[j, rows * d : rows * (d + 1), :] = one_ref[d, rows * j : rows * (j + 1), :]
    piece = 256
    for j in range(parts):
        for n in range(width // piece):
            cols = slice(n * piece, (n + 1) * piece)
            pre = dot(normed_ref[...], win_ref[j, :, cols]) + bin_ref[j, :, cols].astype(wide)
            phi = 0.5 + 0.5 * lax.erf(pre * root_half)
            act_ref[j, :, cols] = (pre * phi).astype(half)
            slope_ref[j, :, cols] = (phi + (pre * slope_const) * jnp.exp2(pre * pre * half_log2e)).astype(half)

    for copy in copies[2]:
        copy.wait()

    def second(j):
        return fc_ref[pl.ds(j * per, per)].reshape(width, width)

    sum_ref[...] = dot(act_ref[0], second(0))

    @pl.loop(1, parts)
    def _(j):
        sum_ref[...] += dot(act_ref[j], second(j))

    d_branch_ref, g_ref = normed_ref, d_pre_ref
    first = second(0)
    for at in tiles:
        r = unit_ref[at, :] * vec[1:2] + vec[2:3] + (sum_ref[at, :] + vec[3:4])
        centred = r - row_mean(r)
        spread = lax.rsqrt(row_mean(centred * centred) + norm_eps)
        unit = centred * spread
        out_ref[at, :] = (unit * vec[4:5] + vec[5:6]).astype(half)
        e = grad_ref[at, :].astype(wide) * vec[4:5]
        d_two = spread * (e - row_mean(e) - unit * row_mean(e * unit))
        sum_ref[at, :] = d_two
        d_branch = d_two.astype(half)
        d_branch_ref[at, :] = d_branch
        d_pre_ref[at, :] = (dot(d_branch, first, NT) * slope_ref[0, at, :].astype(wide)).astype(half)

    outs = [pltpu.make_async_copy(out_ref, out_out, out_sems.at[0])]
    outs[0].start()
    sum_ref[...] += dot(d_pre_ref[...], win_ref[0], NT)

    @pl.loop(1, parts)
    def _(j):
        d_act = dot(d_branch_ref[...], second(j), NT)
        d_pre = (d_act * slope_ref[j].astype(wide)).astype(half)
        sum_ref[...] += dot(d_pre, win_ref[j], NT)

    for i, at in enumerate(tiles):
        unit_one = unit_ref[at, :]
        e = sum_ref[at, :] * vec[1:2]
        d_one = spreads[i] * (e - row_mean(e) - unit_one * row_mean(e * unit_one))
        sum_ref[at, :] = d_one
        d_mixed = dot(d_one.astype(half), wout_ref[...], NT)
        g_ref[at, :] = (d_mixed * inv_ref[at, :]).astype(half)
        outs.append(pltpu.make_async_copy(sum_ref.at[at], d_one_out.at[at], out_sems.at[1 + 2 * i]))
        outs.append(pltpu.make_async_copy(g_ref.at[at], g_out.at[at], out_sems.at[2 + 2 * i]))
        for copy in outs[-2:]:
            copy.start()
    for copy in outs:
        copy.wait()


def feed(me, mixed, x, grad, inv, arrays, specs, counts, table, vec, bias):
    rows, width = x.shape
    devices = table.shape[0]
    parts = bias.shape[0]
    vmem = pltpu.VMEM
    return pl.pallas_call(
        functools.partial(feed_kernel, specs),
        in_specs=[SCALARS, SCALARS] + [NEAR] * 6 + [PLACED] * len(arrays),
        out_specs=[PLACED] * 3,
        out_shape=[shape((rows, width), half), shape((rows, width), wide), shape((rows, width), half)],
        scratch_shapes=[vmem((devices, count, width), half) for count in counts]
        + [
            vmem((parts, width, width), half),
            vmem((width, width), half),
            vmem((rows, width), half),
            vmem((rows, width), wide),
            vmem((parts, rows, width), half),
            vmem((parts, rows, width), half),
            vmem((rows, width), wide),
            vmem((rows, width), half),
            vmem((rows, width), half),
            pltpu.SemaphoreType.DMA((3, devices)),
            pltpu.SemaphoreType.DMA((1 + 2 * (rows // 256),)),
        ],
        compiler_params=params(LIMITS[2]),
        cost_estimate=cost(40),
    )(me, table, vec, bias, mixed, x, grad, inv, *arrays)


def project_back_kernel(d_ref, w_ref, one_ref, d_red_ref, ad_ref, grad_ref):
    grad = one_ref[...] + dot(d_red_ref[...], ad_ref[0:16, :])
    for j in range(3):
        grad += dot(d_ref[j], w_ref[j], NT)
    grad_ref[...] = grad


def project_back(d_qkv, d_one, d_red, wqkv, ad):
    rows, width = d_one.shape
    tile = 512
    block = pl.BlockSpec((tile, width), lambda i: (i, 0))
    return pl.pallas_call(
        project_back_kernel,
        grid=(rows // tile,),
        in_specs=[
            pl.BlockSpec((3, tile, width), lambda i: (0, i, 0)),
            pl.BlockSpec(wqkv.shape, lambda i: (0, 0, 0), pipeline_mode=pl.Buffered(1)),
            block,
            pl.BlockSpec((tile, 16), lambda i: (i, 0)),
            constant(ad.shape),
        ],
        out_specs=block,
        out_shape=shape((rows, width), wide),
        compiler_params=params(LIMITS[4]),
        cost_estimate=cost(8),
    )(*[pltpu.with_memory_space_constraint(t, pltpu.HBM) for t in (d_qkv, wqkv, d_one, d_red)], ad)


def body(
    hidden_in, grad_out, seq_lengths, key_mask, w_qkv, b_qv, w_out, b_out, ln1_gain, ln1_bias,
    w_in, b_in, w_fc, b_fc, ln2_gain, ln2_bias, adapter_weight, adapter_first, adapter_second,
):
    tok_rows, width = hidden_in.shape
    windows = seq_lengths.shape[0]
    length = tok_rows // windows
    rank = ADAPTER_RANK
    own_rows = w_out.shape[0]
    devices = width // own_rows
    ffn_parts = w_in.shape[1] // width
    block_extent = width * rank
    span = adapter_weight.shape[0] // rank
    shards = width // span

    vectors = b_in, b_qv, b_out, ln1_gain, ln1_bias, b_fc, ln2_gain, ln2_bias
    pack_a, pack_b, pack_1 = pack(w_qkv, w_out, w_in, w_fc, adapter_weight, vectors)

    seq_ends = jnp.cumsum(seq_lengths, axis=1)
    positions = jnp.arange(length, dtype=jnp.int32)
    slot_ids = jnp.sum((positions[None, :, None] >= seq_ends[:, None, :]).astype(jnp.int32), axis=2)
    slots = seq_lengths.shape[1]
    lane = jnp.arange(FEAT, dtype=jnp.int32)[None, None, :]
    same = slot_ids[:, :, None] == lane
    padded = (key_mask.reshape(windows, length) == 0)[:, :, None]
    query_feat = jnp.where((lane <= slots) & ~same, 1.0, 0.0).astype(half)
    key_feat = jnp.where(same | ((lane == slots) & padded), masked, 0.0).astype(half)

    staged = devices == 32
    me = lax.axis_index(AXES).astype(jnp.int32).reshape(1)
    split = w_fc.shape[0]
    if staged:
        list_a, state = gather_attention(pack_a, pack_b)
        ring = Ring(state)
    else:
        lists = [[everyone(p, devices)] for p in (pack_a, pack_1[split:], pack_1[:split], w_fc)]
        list_a = lists[0]
    qkv, qkv_far, reduced, factors, vec, bias_in, wqkv = project(me, hidden_in, list_a, ffn_parts, shards)
    before = ()
    if staged:
        ring.step(reduced)
        ring.swap(reduced, 1)
    for w in range(windows):
        before = attend(w, qkv, query_feat, key_feat, before)
        if staged:
            ring.step(before[0])
            ring.swap(before[0], w + 2)
    mixed, inv, probs = before
    if staged:
        ring.end(mixed)
        held = ring.held
        arrays = [h.array for h in held]
        specs = [[(i, start) for i in range(len(held))] for start in (2 * split, split, 0)]
    else:
        held, arrays = lists[1], [h[0].array for h in lists[1:]]
        specs = [[(0, 0)], [(1, 0)], [(2, 0)]]
    counts = pack_1.shape[0] - split, split, split
    hidden_out, d_one, g = feed(
        me, mixed, hidden_in, grad_out, inv, arrays, specs, counts, places(held), vec, bias_in
    )
    d_qkv, d_reduced, partial_grad = attend_back(qkv_far, g, mixed, probs, hidden_in, reduced, factors, devices)
    grad_in = project_back(d_qkv, d_one, d_reduced, wqkv, factors)
    owned = lax.all_to_all(partial_grad, AXES, 0, 0, tiled=True)
    owned_grad = jnp.sum(owned, axis=0).T.reshape(-1)
    shard_len = owned_grad.shape[0]
    flat_place = lax.axis_index(AXES) * shard_len + jnp.arange(shard_len, dtype=jnp.int32)
    step_rates = jnp.where(flat_place >= 2 * block_extent, rate_second, rate_first)
    new_first = beta_one * adapter_first + (1.0 - beta_one) * owned_grad
    new_second = beta_two * adapter_second + (1.0 - beta_two) * owned_grad * owned_grad
    update = (
        new_first
        / (1.0 - beta_one**adam_step)
        / (jnp.sqrt(new_second / (1.0 - beta_two**adam_step)) + adam_eps)
    )
    new_weight = adapter_weight - step_rates * (update + decay_rate * adapter_weight)
    return (hidden_out, grad_in, new_weight, new_first, new_second)


def solution(mesh):
    rows, line = P(AXES, None), P(AXES)
    return jax.shard_map(
        body,
        mesh=mesh,
        in_specs=(
            rows, rows, rows, line, rows, line, rows, line, line, line,
            rows, line, rows, line, line, line, line, line, line,
        ),
        out_specs=(rows, rows, line, line, line),
        check_vma=False,
    )
```

```python
import functools

import jax
import jax.numpy as jnp
import numpy as np
from jax import lax
from jax.experimental import pallas as pl
from jax.experimental.pallas import tpu as pltpu
from jax.sharding import PartitionSpec as P

H = 12
ADAPTER_RANK = 8

norm_eps = 1e-05
low_rank_scale = 2.0
beta_one = 0.9
beta_two = 0.999
adam_eps = 1e-08
adam_step = 100.0
decay_rate = 0.01
rate_first = 0.002
rate_second = 0.032
slope_const = 0.3989422804014327
root_half = 0.7071067811865476
half_log2e = -0.7213475204444817
masked = -1e30

half = jnp.bfloat16
wide = jnp.float32
AXES = ("dp", "group")
WIDTH = 768
PAIR = 128
FEAT = 128

NN = (((1,), (0,)), ((), ()))
NT = (((1,), (1,)), ((), ()))
TN = (((0,), (0,)), ((), ()))


def dot(left, right, dims=NN):
    return lax.dot_general(left, right, dims, preferred_element_type=wide)


LIMITS = 28, 24, 56, 30, 30


def params(mib=58):
    return pltpu.CompilerParams(vmem_limit_bytes=mib * 2**20)


def cost(us):
    return pl.CostEstimate(flops=int(us * 8e8), bytes_accessed=int(us * 2.5e6), transcendentals=0)


def shape(dims, dtype):
    return pltpu.HBM(dims, dtype)


def near(dims, dtype):
    return pltpu.VMEM(dims, dtype)


def row_mean(values):
    return jnp.mean(values, axis=-1, keepdims=True)


class Held:
    def __init__(self, array, owner):
        self.array, self.owner = array, owner

    def send(self, to):
        count = self.owner.shape[0]
        pairs = [(i, to(i)) for i in range(count)]
        owner = np.zeros_like(self.owner)
        for i, j in pairs:
            owner[j] = self.owner[i]
        return Held(lax.ppermute(self.array, AXES, pairs), owner)

    def rows_from(self, start):
        part = Held(self.array, self.owner)
        part.start = start
        return part

    start = 0


def join_after(gate, *held):
    arrays = lax.optimization_barrier((gate, *[h.array for h in held]))[1:]
    return join(*[Held(array, h.owner) for array, h in zip(arrays, held)])


def join(*held):
    return Held(
        jnp.concatenate([h.array for h in held], axis=0), np.concatenate([h.owner for h in held], axis=1)
    )


def after(held, *others):
    first, *_ = lax.optimization_barrier((held.array, *[o.array for o in others]))
    return Held(first, held.owner)


def own(array, devices):
    return Held(array[None], np.arange(devices, dtype=np.int32)[:, None])


def other_core(i):
    return i ^ 1


def first_way(i):
    return i ^ (2 if i % 2 == 0 else 4)


def second_way(i):
    return i ^ (4 if i % 2 == 0 else 2)


def along(i):
    return (i + (8 if i % 2 == 0 else -8)) % 32


def up(i):
    return (i + 8) % 32


def down(i):
    return (i - 8) % 32


def across(i):
    return (i + 16) % 32


def gather_attention(pack_a, pack_b):
    a, b = own(pack_a, 32), own(pack_b, 32)
    close = [a.send(up), a.send(down)]
    ways = a.send(first_way)
    far = far_first = a.send(across)
    b_ways = b.send(first_way)
    a_own = join(a, ways)
    a_own2 = a_own.send(second_way)
    close = join(*close)
    close_ways = close.send(first_way)
    far_ways = far.send(first_way)
    close = join(close, close_ways)
    close2 = close.send(second_way)
    far = join(far, far_ways)
    far2 = far.send(second_way)
    held = [a_own, a_own2, close, far, close2, far2]
    held += [h.send(other_core) for h in held]
    return held, (b, b_ways, far_first, far2)


class Ring:
    def __init__(self, state):
        b, b_ways, far, far2 = state
        gate = far2.array
        self.held = []
        self.now = after(b, far).send(along)
        self.ways = [join_after(gate, b, b_ways)]
        self.seconds = [self.ways[0].send(second_way)]
        self.waiting = []
        self.now = after(self.now, far2)
        self.turn()

    def turn(self):
        arrived = self.now
        self.now = arrived.send(along)
        self.waiting.append((arrived, arrived.send(first_way)))

    def step(self, token):
        if self.waiting:
            pair = join_after(token, *self.waiting.pop())
            self.ways.append(pair)
            self.seconds.append(pair.send(second_way))
            if len(self.ways) == 3:
                self.early = [pair, pair.send(other_core)]
        if self.now is not None:
            self.now = after(self.now, Held(token, None))
            if len(self.ways) < 3:
                self.turn()
            else:
                self.last = [self.now, self.now.send(first_way), self.now.send(second_way)]
                self.now = None

    def end(self, token):
        self.last.append(after(self.last[1], Held(token, None)).send(second_way))
        self.hand_over(token, self.last[:3])
        self.held += [self.last[3], self.last[3].send(other_core)]

    def hand_over(self, token, some):
        arrays = lax.optimization_barrier((token, *[h.array for h in some]))[1:]
        for array, h in zip(arrays, some):
            h = Held(array, h.owner)
            self.held += [h, h.send(other_core)]

    def swap(self, token, count):
        for pair, second in list(zip(self.ways, self.seconds))[len(self.held) // 4 : count]:
            if len(self.held) == 8:
                self.held += self.early
                self.hand_over(token, [second])
            else:
                self.hand_over(token, [pair, second])


def everyone(array, devices):
    owner = np.tile(np.arange(devices, dtype=np.int32), (devices, 1))
    return Held(lax.all_gather(array, AXES, axis=0, tiled=False), owner)


def places(held):
    table = np.concatenate([h.owner for h in held], axis=1)
    assert all(sorted(line) == list(range(len(table))) for line in table)
    return jnp.asarray(table, jnp.int32)


def place_blocks(me_ref, table_ref, block_refs, all_ref):
    me = me_ref[0]
    i = 0
    for ref in block_refs:
        for b in range(ref.shape[0]):
            all_ref[table_ref[me, i]] = ref[b]
            i += 1


SCALARS = pl.BlockSpec(memory_space=pltpu.SMEM)
PLACED = pl.BlockSpec(memory_space=pl.ANY)
NEAR = pl.BlockSpec(memory_space=pltpu.VMEM)


def pack_kernel(span, wqkv_ref, wout_ref, win_ref, wfc_ref, factor_ref, *refs):
    line_refs, (a_ref, b_ref, one_ref) = refs[:-3], refs[-3:]
    rows, width = wout_ref.shape
    for j in range(3):
        a_ref[rows * j : rows * (j + 1), :] = wqkv_ref[:, width * j : width * (j + 1)]
    rank = ADAPTER_RANK
    count = factor_ref.shape[0]
    lane = lax.broadcasted_iota(jnp.int32, (rank, count), 1)
    row = lax.broadcasted_iota(jnp.int32, (rank, count), 0)
    spread = jnp.where(lane % rank == row, factor_ref[...].reshape(1, count).astype(half).astype(wide), 0.0).astype(half)
    place = lax.broadcasted_iota(jnp.int32, (count, PAIR), 0) // rank
    take = (place == lax.broadcasted_iota(jnp.int32, (count, PAIR), 1)).astype(wide).astype(half)
    a_ref[3 * rows :, :PAIR] = dot(spread, take).astype(half)
    a_ref[3 * rows :, PAIR : 2 * PAIR] = jnp.zeros((rank, PAIR), half)
    for i, line in enumerate(LINES):
        at = PAIR
        for k in line:
            n = line_refs[k].shape[0]
            a_ref[3 * rows + i : 3 * rows + i + 1, at : at + n] = line_refs[k][...].reshape(1, n)
            at += n
    a_ref[3 * rows :, 2 * PAIR :] = jnp.zeros((rank, width - 2 * PAIR), half)
    split = wfc_ref.shape[0]
    one_ref[...] = jnp.zeros_like(one_ref)
    for j in range(win_ref.shape[1] // width):
        one_ref[rows * j : rows * (j + 1), :] = win_ref[:, width * j : width * (j + 1)]
    one_ref[split : split + rows, :] = wout_ref[...]
    b_ref[:split, :] = wfc_ref[...]
    b_ref[split:, :] = one_ref[...]


LINES = (0,), (1, 2, 3), (4, 5, 6, 7)


def pack(w_qkv, w_out, w_in, w_fc, factor, vectors):
    rows, width = w_out.shape
    one_rows = w_fc.shape[0] + rows
    one_rows += (-one_rows) % 16
    return pl.pallas_call(
        functools.partial(pack_kernel, factor.shape[0] // ADAPTER_RANK),
        out_shape=[
            jax.ShapeDtypeStruct((3 * rows + ADAPTER_RANK, width), half),
            jax.ShapeDtypeStruct((w_fc.shape[0] + one_rows, width), half),
            jax.ShapeDtypeStruct((one_rows, width), half),
        ],
        compiler_params=params(),
        cost_estimate=cost(2),
    )(w_qkv, w_out, w_in, w_fc, factor, *vectors)


def unfold(pieces, piece, per):
    devices, lanes = pieces.shape[0], pieces.shape[-1]
    rows = pieces.shape[1:-1]
    part = WIDTH // per
    lane = lax.broadcasted_iota(jnp.int32, (lanes, WIDTH), 1)
    row = lax.broadcasted_iota(jnp.int32, (lanes, WIDTH), 0)
    repeat = (lane % part + piece == row).astype(wide).astype(half)
    spread = dot(pieces.reshape(-1, lanes), repeat).reshape(devices // per, per, *rows, WIDTH)
    dims = (per, *rows, WIDTH)
    shard = lax.broadcasted_iota(jnp.int32, dims, 0)
    place = lax.broadcasted_iota(jnp.int32, dims, len(dims) - 1) // part
    return jnp.sum(jnp.where((shard == place)[None], spread, 0.0), axis=1)


def project_kernel(blocks, shards, me_ref, table_ref, x_ref, *refs):
    block_refs = refs[:blocks]
    qkv_ref, far_ref, red_ref, ad_ref, vec_ref, bin_ref, wout_ref, ga_ref, w_ref, bias_ref, sem, sems = refs[blocks:]
    devices = ga_ref.shape[0]
    width = x_ref.shape[1]
    rows = width // devices
    keep = pltpu.make_async_copy(w_ref, wout_ref, sem)

    @pl.when(pl.program_id(0) == 0)
    def _():
        place_blocks(me_ref, table_ref, block_refs, ga_ref)
        for d in range(devices):
            span = slice(rows * d, rows * d + rows)
            for j in range(3):
                w_ref[j, span, :] = ga_ref[d, rows * j : rows * (j + 1), :]
        keep.start()
        small = ga_ref[:, 3 * rows :, :PAIR]
        lines = [ga_ref[:, 3 * rows + i, PAIR : 2 * PAIR] for i in range(3)]
        ad_ref[...] = unfold(small, 0, shards).reshape(4 * ADAPTER_RANK, width).astype(half)
        line = unfold(lines[0], 0, shards).astype(half)
        for j in range(bin_ref.shape[0]):
            bin_ref[j] = line[j : j + 1]
        bias = unfold(lines[1], 0, devices // 2)
        bias_ref[0], bias_ref[1], bias_ref[2] = bias[0:1], jnp.zeros_like(bias[0:1]), bias[1:2]
        vecs = [unfold(lines[1], rows * j, devices) for j in (2, 3)]
        vecs += [unfold(lines[2], rows * j, devices) for j in range(4)]
        vec_ref[...] = jnp.concatenate(vecs + vecs[:2], axis=0)

        red_ref[...] = dot(x_ref[...], ad_ref[0:16, :], NT).astype(half)

    j = pl.program_id(0)
    reduced = red_ref[...]
    lane = lax.broadcasted_iota(jnp.int32, reduced.shape, 1)
    own_lanes = jnp.where(lane // 8 * 2 == j, reduced, jnp.zeros_like(reduced))
    wide_row = dot(x_ref[...], w_ref[j]) + bias_ref[j]
    wide_row += low_rank_scale * dot(own_lanes, ad_ref[16:32, :])
    scale = jnp.where(j == 0, 0.125, 1.0)
    qkv_ref[j] = (wide_row.astype(half).astype(wide) * scale).astype(half)
    pltpu.make_async_copy(qkv_ref.at[j], far_ref.at[j], sems.at[j]).start()

    @pl.when(j == pl.num_programs(0) - 1)
    def _():
        keep.wait()
        for i in range(3):
            pltpu.make_async_copy(qkv_ref.at[i], far_ref.at[i], sems.at[i]).wait()


def constant(dims):
    return pl.BlockSpec(dims, lambda i: (0,) * len(dims))


def project(me, x, held, parts, shards):
    rows, width = x.shape
    devices = held[0].owner.shape[0]
    return pl.pallas_call(
        functools.partial(project_kernel, len(held), shards),
        grid=(3,),
        in_specs=[SCALARS, SCALARS, NEAR] + [NEAR] * len(held),
        out_specs=[
            NEAR,
            PLACED,
            constant((rows, 16)),
            constant((4 * ADAPTER_RANK, width)),
            constant((8, width)),
            constant((parts, 1, width)),
            PLACED,
        ],
        out_shape=[
            near((3, rows, width), half),
            shape((3, rows, width), half),
            shape((rows, 16), half),
            shape((4 * ADAPTER_RANK, width), half),
            shape((8, width), wide),
            shape((parts, 1, width), half),
            shape((3, width, width), half),
        ],
        scratch_shapes=[
            pltpu.VMEM((devices, 3 * (width // devices) + ADAPTER_RANK, width), half),
            pltpu.VMEM((3, width, width), half),
            pltpu.VMEM((3, 1, width), wide),
            pltpu.SemaphoreType.DMA,
            pltpu.SemaphoreType.DMA((3,)),
        ],
        compiler_params=params(LIMITS[0]),
        cost_estimate=cost(8),
    )(me, places(held), x, *[h.array for h in held])


STEP = 2


def low_lanes(length):
    return lax.broadcasted_iota(jnp.int32, (length, PAIR), 1) < 64


def apart(pair, low):
    zero = jnp.zeros_like(pair)
    return jnp.concatenate([jnp.where(low, pair, zero), jnp.where(low, zero, pair)], axis=0)


def together(heads, low):
    length = low.shape[0]
    return jnp.where(low, heads[:length], heads[length:])


def attend_kernel(q_ref, k_ref, v_ref, fq_ref, fk_ref, *refs):
    mixed_ref, inv_ref, p_ref = refs[-3:]
    length = q_ref.shape[1]
    low = low_lanes(length)
    one = jnp.ones((length, PAIR), half)
    fq = jnp.concatenate([fq_ref[0], fq_ref[0]], axis=0)

    def scores_of(i):
        lanes = slice(i * PAIR, (i + 1) * PAIR)
        queries = jnp.concatenate([apart(q_ref[0, :, lanes], low), fq], axis=1)
        keys = jnp.concatenate([k_ref[0, :, lanes], fk_ref[0]], axis=1)
        return dot(queries, keys, NT)

    scores = [scores_of(i) for i in range(STEP)]
    for i in range(STEP):
        lanes = slice(i * PAIR, (i + 1) * PAIR)
        highest = jnp.max(scores[i], axis=1, keepdims=True)
        p = jnp.exp(scores[i] - highest).astype(half)
        p_ref[0, i] = p
        total = dot(p, jnp.concatenate([v_ref[0, :, lanes], one], axis=1))
        inv = together(1.0 / total[:, PAIR:], low)
        mixed_ref[:, lanes] = (together(total[:, :PAIR], low) * inv).astype(half)
        inv_ref[:, lanes] = inv


def attend(window, qkv, fq, fk, before):
    _, rows, width = qkv.shape
    windows, length, _ = fq.shape
    pairs = width // PAIR
    block = pl.BlockSpec((length, STEP * PAIR), lambda h: (window, h))
    feat = pl.BlockSpec((1, length, FEAT), lambda h: (window, 0, 0))
    heads = [pl.BlockSpec((1, length, STEP * PAIR), lambda h, j=j: (j, window, h)) for j in range(3)]
    return pl.pallas_call(
        attend_kernel,
        grid=(pairs // STEP,),
        in_specs=heads + [feat, feat] + [PLACED] * len(before),
        out_specs=[block, block, pl.BlockSpec((1, STEP, 2 * length, length), lambda h: (window, h, 0, 0))],
        out_shape=[
            shape((rows, width), half),
            shape((rows, width), wide),
            shape((windows, pairs, 2 * length, length), half),
        ],
        input_output_aliases={5 + i: i for i in range(len(before))},
        compiler_params=params(LIMITS[1]),
        cost_estimate=cost(6),
    )(qkv, qkv, qkv, fq, fk, *before)


def attend_back_kernel(
    q_ref, k_ref, v_ref, g_ref, mixed_ref, p_ref, x_ref, red_ref, ad_ref, d_ref, d_red_ref, out_ref, sum_ref, keep_ref
):
    length = q_ref.shape[1]
    low = low_lanes(length)
    w, h = pl.program_id(0), pl.program_id(1)
    last = h == pl.num_programs(1) - 1

    def d_probs_of(i):
        lanes = slice(i * PAIR, (i + 1) * PAIR)
        g2 = g_ref[:, lanes]
        prod = g2.astype(wide) * mixed_ref[:, lanes].astype(wide)
        centre = jnp.sum(apart(prod, low), axis=1, keepdims=True)
        return dot(apart(g2, low), v_ref[0, :, lanes], NT), centre

    d_probs = [d_probs_of(i) for i in range(STEP)]
    for i in range(STEP):
        lanes = slice(i * PAIR, (i + 1) * PAIR)
        p = p_ref[0, i]
        raw, centre = d_probs[i]
        ds = (p.astype(wide) * (raw - centre)).astype(half)
        q_t, g_t = q_ref[0, :, lanes].T, g_ref[:, lanes].T

        def own_rows(left, both):
            return jnp.concatenate(
                [dot(left, both[n * length : (n + 1) * length])[64 * n : 64 * n + 64] for n in range(2)], axis=0
            )

        dv = own_rows(g_t, p).astype(half).T
        dk = own_rows(q_t, ds).astype(half).T
        dq = (together(dot(ds, k_ref[0, :, lanes]), low) * 0.125).astype(half)
        d_ref[0, :, lanes] = dq
        d_ref[1, :, lanes] = dk
        d_ref[2, :, lanes] = dv
        cols = pl.ds(pl.multiple_of((h * STEP + i) * PAIR, PAIR), PAIR)
        keep_ref[0, :, cols] = dq
        keep_ref[1, :, cols] = dv

    @pl.when(last)
    def _():
        dq, dv = keep_ref[0], keep_ref[1]
        up, red = ad_ref[16:32, :], red_ref[...]
        row = lax.broadcasted_iota(jnp.int32, up.shape, 0)
        none = jnp.zeros_like(up)
        d_red = dot(dq, jnp.where(row < 8, up, none), NT) + dot(dv, jnp.where(row < 8, none, up), NT)
        d_red = (low_rank_scale * d_red).astype(half)
        d_red_ref[...] = d_red
        grad = jnp.concatenate(
            [
                dot(d_red, x_ref[...], TN),
                low_rank_scale * dot(red, dq, TN)[0:8],
                low_rank_scale * dot(red, dv, TN)[8:16],
            ],
            axis=0,
        )

        @pl.when(w == 0)
        def _():
            sum_ref[...] = grad

        @pl.when(w > 0)
        def _():
            sum_ref[...] += grad

    @pl.when(last & (w == pl.num_programs(0) - 1))
    def _():
        devices, rank, span = out_ref.shape
        shards = sum_ref.shape[1] // span
        for d in range(devices):
            m, i = d // shards, d % shards
            out_ref[d] = sum_ref[m * rank : (m + 1) * rank, i * span : (i + 1) * span]


def attend_back(qkv, g, mixed, p, x, red, ad, devices):
    _, rows, width = qkv.shape
    windows, pairs, _, length = p.shape
    block = pl.BlockSpec((length, STEP * PAIR), lambda w, h: (w, h))
    heads = [pl.BlockSpec((1, length, STEP * PAIR), lambda w, h, j=j: (j, w, h)) for j in range(3)]
    thin = pl.BlockSpec((length, 16), lambda w, h: (w, 0))
    out = (devices, ADAPTER_RANK, 4 * width // devices)
    return pl.pallas_call(
        attend_back_kernel,
        grid=(windows, pairs // STEP),
        in_specs=heads
        + [
            block,
            block,
            pl.BlockSpec((1, STEP, 2 * length, length), lambda w, h: (w, h, 0, 0)),
            pl.BlockSpec((length, width), lambda w, h: (w, 0)),
            thin,
            pl.BlockSpec(ad.shape, lambda w, h: (0, 0)),
        ],
        out_specs=[
            pl.BlockSpec((3, length, STEP * PAIR), lambda w, h: (0, w, h)),
            thin,
            pl.BlockSpec(out, lambda w, h: (0, 0, 0)),
        ],
        out_shape=[shape((3, rows, width), half), shape((rows, 16), half), shape(out, wide)],
        scratch_shapes=[pltpu.VMEM((4 * ADAPTER_RANK, width), wide), pltpu.VMEM((2, length, width), half)],
        compiler_params=params(LIMITS[3]),
        cost_estimate=cost(20),
    )(*[pltpu.with_memory_space_constraint(t, pltpu.HBM) for t in (qkv, qkv, qkv, g, mixed, p, x)], red, ad)


def feed_kernel(specs, me_ref, table_ref, vec_ref, bin_ref, mixed_ref, x_ref, grad_ref, inv_ref, *refs):
    arrays = 1 + max(i for spec in specs for i, _ in spec)
    block_refs = refs[:arrays]
    out_out, d_one_out, g_out = refs[arrays : arrays + 3]
    (
        wo_ref, one_ref, fc_ref, win_ref, wout_ref,
        normed_ref, unit_ref, act_ref, slope_ref, sum_ref, out_ref, d_pre_ref, sems, out_sems,
    ) = refs[arrays + 3 :]
    devices = fc_ref.shape[0]
    rows_all, width = x_ref.shape
    parts = win_ref.shape[0]
    per = devices // parts
    rows = width // devices
    me = me_ref[0]
    copies = []
    for n, (target, spec) in enumerate(zip((wo_ref, one_ref, fc_ref), specs)):
        count = target.shape[1]
        some = []
        for k, start in spec:
            ref = block_refs[k]
            for b in range(ref.shape[0]):
                source = ref.at[b] if ref.shape[1] == count else ref.at[b, pl.ds(start, count)]
                i = len(some)
                some.append(pltpu.make_async_copy(source, target.at[table_ref[me, i]], sems.at[n, i]))
        copies.append(some)
    for copy in copies[0]:
        copy.start()
    vec = vec_ref[...]
    tile = 256
    tiles = [slice(t, t + tile) for t in range(0, rows_all, tile)]
    for copy in copies[0]:
        copy.wait()
    for copy in copies[1]:
        copy.start()
    for d in range(devices):
        wout_ref[rows * d : rows * (d + 1), :] = wo_ref[d, 0:rows, :]
    spreads = []
    for at in tiles:
        r = x_ref[at, :].astype(wide) + (dot(mixed_ref[at, :], wout_ref[...]) + vec[0:1])
        centred = r - row_mean(r)
        spread = lax.rsqrt(row_mean(centred * centred) + norm_eps)
        spreads.append(spread)
        unit = centred * spread
        unit_ref[at, :] = unit
        normed_ref[at, :] = (unit * vec[1:2] + vec[2:3]).astype(half)
    for copy in copies[1]:
        copy.wait()
    for copy in copies[2]:
        copy.start()
    for d in range(devices):
        for j in range(parts):
            win_ref[j, rows * d : rows * (d + 1), :] = one_ref[d, rows * j : rows * (j + 1), :]
    piece = 256
    for j in range(parts):
        for n in range(width // piece):
            cols = slice(n * piece, (n + 1) * piece)
            pre = dot(normed_ref[...], win_ref[j, :, cols]) + bin_ref[j, :, cols].astype(wide)
            phi = 0.5 + 0.5 * lax.erf(pre * root_half)
            act_ref[j, :, cols] = (pre * phi).astype(half)
            slope_ref[j, :, cols] = (phi + (pre * slope_const) * jnp.exp2(pre * pre * half_log2e)).astype(half)

    for copy in copies[2]:
        copy.wait()

    def second(j):
        return fc_ref[pl.ds(j * per, per)].reshape(width, width)

    sum_ref[...] = dot(act_ref[0], second(0))

    @pl.loop(1, parts)
    def _(j):
        sum_ref[...] += dot(act_ref[j], second(j))

    d_branch_ref, g_ref = normed_ref, d_pre_ref
    first = second(0)
    for at in tiles:
        r = unit_ref[at, :] * vec[1:2] + vec[2:3] + (sum_ref[at, :] + vec[3:4])
        centred = r - row_mean(r)
        spread = lax.rsqrt(row_mean(centred * centred) + norm_eps)
        unit = centred * spread
        out_ref[at, :] = (unit * vec[4:5] + vec[5:6]).astype(half)
        e = grad_ref[at, :].astype(wide) * vec[4:5]
        d_two = spread * (e - row_mean(e) - unit * row_mean(e * unit))
        sum_ref[at, :] = d_two
        d_branch = d_two.astype(half)
        d_branch_ref[at, :] = d_branch
        d_pre_ref[at, :] = (dot(d_branch, first, NT) * slope_ref[0, at, :].astype(wide)).astype(half)

    outs = [pltpu.make_async_copy(out_ref, out_out, out_sems.at[0])]
    outs[0].start()
    sum_ref[...] += dot(d_pre_ref[...], win_ref[0], NT)

    @pl.loop(1, parts)
    def _(j):
        d_act = dot(d_branch_ref[...], second(j), NT)
        d_pre = (d_act * slope_ref[j].astype(wide)).astype(half)
        sum_ref[...] += dot(d_pre, win_ref[j], NT)

    for i, at in enumerate(tiles):
        unit_one = unit_ref[at, :]
        e = sum_ref[at, :] * vec[1:2]
        d_one = spreads[i] * (e - row_mean(e) - unit_one * row_mean(e * unit_one))
        sum_ref[at, :] = d_one
        d_mixed = dot(d_one.astype(half), wout_ref[...], NT)
        g_ref[at, :] = (d_mixed * inv_ref[at, :]).astype(half)
        outs.append(pltpu.make_async_copy(sum_ref.at[at], d_one_out.at[at], out_sems.at[1 + 2 * i]))
        outs.append(pltpu.make_async_copy(g_ref.at[at], g_out.at[at], out_sems.at[2 + 2 * i]))
        for copy in outs[-2:]:
            copy.start()
    for copy in outs:
        copy.wait()


def feed(me, mixed, x, grad, inv, arrays, specs, counts, table, vec, bias):
    rows, width = x.shape
    devices = table.shape[0]
    parts = bias.shape[0]
    vmem = pltpu.VMEM
    return pl.pallas_call(
        functools.partial(feed_kernel, specs),
        in_specs=[SCALARS, SCALARS] + [NEAR] * 6 + [PLACED] * len(arrays),
        out_specs=[PLACED] * 3,
        out_shape=[shape((rows, width), half), shape((rows, width), wide), shape((rows, width), half)],
        scratch_shapes=[vmem((devices, count, width), half) for count in counts]
        + [
            vmem((parts, width, width), half),
            vmem((width, width), half),
            vmem((rows, width), half),
            vmem((rows, width), wide),
            vmem((parts, rows, width), half),
            vmem((parts, rows, width), half),
            vmem((rows, width), wide),
            vmem((rows, width), half),
            vmem((rows, width), half),
            pltpu.SemaphoreType.DMA((3, devices)),
            pltpu.SemaphoreType.DMA((1 + 2 * (rows // 256),)),
        ],
        compiler_params=params(LIMITS[2]),
        cost_estimate=cost(40),
    )(me, table, vec, bias, mixed, x, grad, inv, *arrays)


def project_back_kernel(d_ref, w_ref, one_ref, d_red_ref, ad_ref, grad_ref):
    grad = one_ref[...] + dot(d_red_ref[...], ad_ref[0:16, :])
    for j in range(3):
        grad += dot(d_ref[j], w_ref[j], NT)
    grad_ref[...] = grad


def project_back(d_qkv, d_one, d_red, wqkv, ad):
    rows, width = d_one.shape
    tile = 512
    block = pl.BlockSpec((tile, width), lambda i: (i, 0))
    return pl.pallas_call(
        project_back_kernel,
        grid=(rows // tile,),
        in_specs=[
            pl.BlockSpec((3, tile, width), lambda i: (0, i, 0)),
            pl.BlockSpec(wqkv.shape, lambda i: (0, 0, 0), pipeline_mode=pl.Buffered(1)),
            block,
            pl.BlockSpec((tile, 16), lambda i: (i, 0)),
            constant(ad.shape),
        ],
        out_specs=block,
        out_shape=shape((rows, width), wide),
        compiler_params=params(LIMITS[4]),
        cost_estimate=cost(8),
    )(*[pltpu.with_memory_space_constraint(t, pltpu.HBM) for t in (d_qkv, wqkv, d_one, d_red)], ad)


def body(
    hidden_in, grad_out, seq_lengths, key_mask, w_qkv, b_qv, w_out, b_out, ln1_gain, ln1_bias,
    w_in, b_in, w_fc, b_fc, ln2_gain, ln2_bias, adapter_weight, adapter_first, adapter_second,
):
    tok_rows, width = hidden_in.shape
    windows = seq_lengths.shape[0]
    length = tok_rows // windows
    rank = ADAPTER_RANK
    own_rows = w_out.shape[0]
    devices = width // own_rows
    ffn_parts = w_in.shape[1] // width
    block_extent = width * rank
    span = adapter_weight.shape[0] // rank
    shards = width // span

    vectors = b_in, b_qv, b_out, ln1_gain, ln1_bias, b_fc, ln2_gain, ln2_bias
    pack_a, pack_b, pack_1 = pack(w_qkv, w_out, w_in, w_fc, adapter_weight, vectors)

    seq_ends = jnp.cumsum(seq_lengths, axis=1)
    positions = jnp.arange(length, dtype=jnp.int32)
    slot_ids = jnp.sum((positions[None, :, None] >= seq_ends[:, None, :]).astype(jnp.int32), axis=2)
    slots = seq_lengths.shape[1]
    lane = jnp.arange(FEAT, dtype=jnp.int32)[None, None, :]
    same = slot_ids[:, :, None] == lane
    padded = (key_mask.reshape(windows, length) == 0)[:, :, None]
    query_feat = jnp.where((lane <= slots) & ~same, 1.0, 0.0).astype(half)
    key_feat = jnp.where(same | ((lane == slots) & padded), masked, 0.0).astype(half)

    staged = devices == 32
    me = lax.axis_index(AXES).astype(jnp.int32).reshape(1)
    split = w_fc.shape[0]
    if staged:
        list_a, state = gather_attention(pack_a, pack_b)
        ring = Ring(state)
    else:
        lists = [[everyone(p, devices)] for p in (pack_a, pack_1[split:], pack_1[:split], w_fc)]
        list_a = lists[0]
    qkv, qkv_far, reduced, factors, vec, bias_in, wqkv = project(me, hidden_in, list_a, ffn_parts, shards)
    before = ()
    if staged:
        ring.step(reduced)
        ring.swap(reduced, 1)
    for w in range(windows):
        before = attend(w, qkv, query_feat, key_feat, before)
        if staged:
            ring.step(before[0])
            ring.swap(before[0], w + 2)
    mixed, inv, probs = before
    if staged:
        ring.end(mixed)
        held = ring.held
        arrays = [h.array for h in held]
        specs = [[(i, start) for i in range(len(held))] for start in (2 * split, split, 0)]
    else:
        held, arrays = lists[1], [h[0].array for h in lists[1:]]
        specs = [[(0, 0)], [(1, 0)], [(2, 0)]]
    counts = pack_1.shape[0] - split, split, split
    hidden_out, d_one, g = feed(
        me, mixed, hidden_in, grad_out, inv, arrays, specs, counts, places(held), vec, bias_in
    )
    d_qkv, d_reduced, partial_grad = attend_back(qkv_far, g, mixed, probs, hidden_in, reduced, factors, devices)
    grad_in = project_back(d_qkv, d_one, d_reduced, wqkv, factors)
    owned = lax.all_to_all(partial_grad, AXES, 0, 0, tiled=True)
    owned_grad = jnp.sum(owned, axis=0).T.reshape(-1)
    shard_len = owned_grad.shape[0]
    flat_place = lax.axis_index(AXES) * shard_len + jnp.arange(shard_len, dtype=jnp.int32)
    step_rates = jnp.where(flat_place >= 2 * block_extent, rate_second, rate_first)
    new_first = beta_one * adapter_first + (1.0 - beta_one) * owned_grad
    new_second = beta_two * adapter_second + (1.0 - beta_two) * owned_grad * owned_grad
    update = (
        new_first
        / (1.0 - beta_one**adam_step)
        / (jnp.sqrt(new_second / (1.0 - beta_two**adam_step)) + adam_eps)
    )
    new_weight = adapter_weight - step_rates * (update + decay_rate * adapter_weight)
    return (hidden_out, grad_in, new_weight, new_first, new_second)


def solution(mesh):
    rows, line = P(AXES, None), P(AXES)
    return jax.shard_map(
        body,
        mesh=mesh,
        in_specs=(
            rows, rows, rows, line, rows, line, rows, line, line, line,
            rows, line, rows, line, line, line, line, line, line,
        ),
        out_specs=(rows, rows, line, line, line),
        check_vma=False,
    )
```
